512 devices in a mesh: wrk: 32 (over x, y, core), emp: 16 (over z).
Axes of the slice: x: 4, y: 4, z: 16, core: 2. Of those that a mesh axis runs over, the one named last changes fastest.
Arguments:
- worker_emb: bfloat16 [524288, 256], P(('wrk', 'emp')), may hold values from -6 to 6
- employer_emb: bfloat16 [256, 131072], P('wrk', 'emp'), may hold values from -6 to 6
- eligible: int32 [512, 512], P('wrk', 'emp'), may hold values from 0 to 1, as said below
- worker_mass: float32 [524288], P('wrk'), may hold values from 0.5 to 2
- employer_mass: float32 [131072], P('emp'), may hold values from 0.5 to 2
Outputs:
- worker_potential: float32 [524288], P('wrk')
- employer_potential: float32 [131072], P('emp')
The draws below stay inside these ranges and needn't reach their ends.
Inputs may be any that keep to these rules, and one draw needn't show every extreme that they name: eligible holds 0 or 1. The 16 x 32 sub-block of one device (block rows of one index of wrk, block columns of one index of emp) holds at most 12 ones, and some device holds exactly 12. Every block row and every block column holds at least one one.
All inputs are finite; a program needn't handle non-finite values.
Results may differ from the reference program's by a relative error of at most 0.0003.
Values may be sent and summed in bfloat16 or wider, within the bound.
A program may use at most 64 MiB of HBM per device.

```python
import math
import jax
import jax.numpy as jnp
from jax import lax

E = 256
RW = 1024
RE = 256
BW_DEV = 16
BE_DEV = 32
CAP = 12
ITERS = 3
BLOCKS_W = 512
BLOCKS_E = 512
NW = 524288
NE = 131072


cluster_count = 8


noise_level = 0.3


def shared_centers(key):
    return jax.random.normal(jax.random.fold_in(key, 907), (cluster_count, E), jnp.float32)


def draw_worker_emb(key, part):
    centers = shared_centers(key)
    key = jax.random.fold_in(key, 21)
    sub_keys = jax.random.split(key, 3)
    pick_one = jax.random.randint(sub_keys[0], (NW,), 0, cluster_count)
    pick_two = jax.random.randint(sub_keys[1], (NW,), 0, cluster_count)
    cluster_ids = jnp.minimum(pick_one, pick_two)
    jitter = noise_level * jax.random.normal(sub_keys[2], (NW, E), jnp.float32)
    values = centers[cluster_ids] + jitter
    return jnp.clip(values, -6.0, 6.0).astype(jnp.bfloat16)


def draw_employer_emb(key, part):
    centers = shared_centers(key)
    key = jax.random.fold_in(key, 33)
    sub_keys = jax.random.split(key, 3)
    pick_one = jax.random.randint(sub_keys[0], (NE,), 0, cluster_count)
    pick_two = jax.random.randint(sub_keys[1], (NE,), 0, cluster_count)
    cluster_ids = jnp.maximum(pick_one, pick_two)
    jitter = noise_level * jax.random.normal(sub_keys[2], (NE, E), jnp.float32)
    values = centers[cluster_ids] + jitter
    return jnp.clip(values, -6.0, 6.0).T.astype(jnp.bfloat16)


def draw_eligible(key, part):
    key = jax.random.fold_in(key, 11)
    n_wrk = BLOCKS_W // BW_DEV
    n_emp = BLOCKS_E // BE_DEV
    devices_all = n_wrk * n_emp
    slots = BW_DEV * BE_DEV
    keys = jax.random.split(key, 6)
    first = jax.random.randint(keys[0], (devices_all,), 1, CAP + 1)
    second = jax.random.randint(keys[1], (devices_all,), 1, CAP + 1)
    counts = jnp.minimum(first, second)
    busiest = jax.random.randint(keys[2], (), 0, devices_all)
    counts = jnp.where(jnp.arange(devices_all) == busiest, CAP, counts)
    row_coverage = BW_DEV // n_emp
    col_cover = BE_DEV // n_wrk
    base_count = max(row_coverage, col_cover)
    counts = jnp.maximum(counts, base_count)
    shift_row = jax.random.randint(keys[3], (), 0, n_emp)
    shift_col = jax.random.randint(keys[4], (), 0, n_wrk)
    device_ids = jnp.arange(devices_all)
    group_w = device_ids // n_emp
    group_e = device_ids % n_emp
    steps = jnp.arange(base_count)
    local_row = ((group_e + shift_row) % n_emp)[:, None] + n_emp * (steps % row_coverage)[None, :]
    local_col = ((group_w + shift_col) % n_wrk)[:, None] + n_wrk * (steps % col_cover)[None, :]
    base_slot = local_row * BE_DEV + local_col
    slot_ids = jnp.arange(slots)
    is_base = jnp.any(base_slot[:, :, None] == slot_ids[None, None, :], axis=1)
    perm_keys = jax.random.split(keys[5], devices_all)
    perms = jax.vmap(lambda one: jax.random.permutation(one, slots))(perm_keys)
    scores = jnp.where(is_base, perms - slots, perms)
    ranks = jnp.argsort(jnp.argsort(scores, axis=1), axis=1)
    chosen = (ranks < counts[:, None]).astype(jnp.int32)
    pattern = chosen.reshape(n_wrk, n_emp, BW_DEV, BE_DEV).transpose(0, 2, 1, 3)
    return pattern.reshape(BLOCKS_W, BLOCKS_E).astype(jnp.int32)


def steps_of(key, extent, shards, low, top_value):
    gain, own = 1.0, jax.random.fold_in(key, 6)
    for axis_at, shards_of in shards:
        steps = jnp.exp(jax.random.uniform(jax.random.fold_in(own, axis_at), (shards_of,), jnp.float32, low / len(shards), top_value / len(shards)))
        gain = gain * jnp.repeat(steps, extent[axis_at] // shards_of).reshape([-1 if axis == axis_at else 1 for axis in range(len(extent))])
    return gain


def setup_inputs(seed: int = 0) -> dict:
    arg_keys = jax.random.split(jax.random.key(seed), 6)
    worker_emb = draw_worker_emb(jax.random.fold_in(arg_keys[5], 71), 0)
    employer_emb = draw_employer_emb(jax.random.fold_in(arg_keys[5], 71), 0)
    eligible = draw_eligible(jax.random.fold_in(arg_keys[5], 71), 0)
    worker_mass = jnp.clip(jnp.exp(math.log(2.0) - 1.3862944 * jax.random.uniform(arg_keys[3], (NW,), jnp.float32) ** steps_of(arg_keys[3], (NW,), ((0, 32),), -0.2, 0.2)), 0.5, 2.0)
    employer_mass = jnp.clip(jnp.exp(math.log(2.0) - 1.3862944 * jax.random.uniform(arg_keys[4], (NE,), jnp.float32) ** steps_of(arg_keys[4], (NE,), ((0, 16),), -0.2, 0.2)), 0.5, 2.0)
    return dict(worker_emb=worker_emb, employer_emb=employer_emb, eligible=eligible, worker_mass=worker_mass, employer_mass=employer_mass)


SOFTMAX_TEMP = 0.25
EPSILON = 1e-06

def reference(worker_emb, employer_emb, eligible, worker_mass, employer_mass):
    n_wrk = BLOCKS_W // BW_DEV
    n_emp = BLOCKS_E // BE_DEV
    grid = eligible.reshape(n_wrk, BW_DEV, n_emp, BE_DEV).transpose(0, 2, 1, 3).reshape(n_wrk * n_emp, BW_DEV * BE_DEV)
    slot_order = jnp.argsort(1 - grid, axis=1, stable=True)[:, :CAP].astype(jnp.int32)
    usable = jnp.take_along_axis(grid, slot_order, axis=1).astype(jnp.float32)
    device_ids = jnp.arange(n_wrk * n_emp, dtype=jnp.int32)
    row_index = (device_ids // n_emp * BW_DEV)[:, None] + slot_order // BE_DEV
    col_index = (device_ids % n_emp * BE_DEV)[:, None] + slot_order % BE_DEV
    worker_float = worker_emb.astype(jnp.float32)
    inv_worker = lax.rsqrt(lax.optimization_barrier(jnp.mean(worker_float * worker_float, axis=1)) + EPSILON)
    employer_float = employer_emb.astype(jnp.float32)
    inv_employer = lax.rsqrt(lax.optimization_barrier(jnp.mean(employer_float * employer_float, axis=0)) + EPSILON)
    worker_blocks = worker_emb.reshape(BLOCKS_W, RW, E)
    employer_blocks = employer_emb.reshape(E, BLOCKS_E, RE).transpose(1, 0, 2)
    worker_scale = inv_worker.reshape(BLOCKS_W, RW)
    employer_scale = inv_employer.reshape(BLOCKS_E, RE)

    def build(packed):
        row_pick, col_pick, keep_mask = packed
        row_slab = worker_blocks[row_pick].astype(jnp.float32)
        col_slab = employer_blocks[col_pick].astype(jnp.float32)
        cosine_similarity = jnp.einsum('cre,cek->crk', row_slab, col_slab, precision=lax.Precision.HIGHEST)
        cosine_similarity = cosine_similarity * worker_scale[row_pick][:, :, None] * employer_scale[col_pick][:, None, :] / E
        return (jnp.exp((cosine_similarity - 1.0) / SOFTMAX_TEMP) * keep_mask[:, None, None]).astype(jnp.bfloat16)
    tiles = lax.map(build, (row_index, col_index, usable))

    def row_terms(packed):
        return jnp.einsum('crk,ck->cr', packed[0].astype(jnp.float32), packed[1], precision=lax.Precision.HIGHEST)

    def col_terms(packed):
        return jnp.einsum('crk,cr->ck', packed[0].astype(jnp.float32), packed[1], precision=lax.Precision.HIGHEST)
    employer_scaling = jnp.ones((NE,), jnp.float32)
    worker_scaling = jnp.ones((NW,), jnp.float32)
    for step in range(ITERS):
        col_vectors = employer_scaling.reshape(BLOCKS_E, RE)[col_index]
        row_part = lax.map(row_terms, (tiles, col_vectors))
        row_total = jnp.zeros((BLOCKS_W, RW), jnp.float32).at[row_index].add(row_part).reshape(NW)
        worker_scaling = worker_mass / row_total
        row_embedding_vectors = worker_scaling.reshape(BLOCKS_W, RW)[row_index]
        col_part = lax.map(col_terms, (tiles, row_embedding_vectors))
        column_total = jnp.zeros((BLOCKS_E, RE), jnp.float32).at[col_index].add(col_part).reshape(NE)
        employer_scaling = employer_mass / column_total
    return (SOFTMAX_TEMP * jnp.log(worker_scaling), SOFTMAX_TEMP * jnp.log(employer_scaling))
```

```python
import functools

import jax
import jax.numpy as jnp
from jax import lax
from jax.experimental import pallas as pl
from jax.experimental.pallas import tpu as pltpu
from jax.sharding import PartitionSpec as P

E = 256
ITERS = 3
SOFTMAX_TEMP = 0.25
EPSILON = 1e-06
RW = 1024
RE = 256
SLOTS = (16, 48)
CHUNKS = 4
MESH = pl.DeviceIdType.MESH
VMEM = pl.BlockSpec(memory_space=pltpu.VMEM)
SMEM = pl.BlockSpec(memory_space=pltpu.SMEM)
ANY = pl.BlockSpec(memory_space=pl.ANY)
DMA = pltpu.SemaphoreType.DMA


def place():
    w, z = lax.axis_index("wrk"), lax.axis_index("emp")
    return w // 8, lax.rem(w // 2, 4), lax.rem(w, 2), z // 4, lax.rem(z, 4)


def device(x, y, c, z):
    return ((lax.rem(x, 4) * 4 + lax.rem(y, 4)) * 2 + c, lax.rem(z, 16))


def remote(src, dst, send, recv, to):
    return pltpu.make_async_remote_copy(
        src_ref=src, dst_ref=dst, send_sem=send, recv_sem=recv, device_id=to, device_id_type=MESH
    )


def took(ref, sem):
    pltpu.make_async_copy(ref, ref, sem).wait()


def gather_kernel(
    wk, em, small,
    rows, cols, small_out, peak_out,
    small_all, top, top_z, top_w,
    keep_sem, z_send, z_recv, xy_send, xy_recv, core_send, core_recv,
    row_send, row_recv, small_send, small_recv, top_send, top_recv,
):
    x, y, c, a, b = place()
    w, z = lax.axis_index("wrk"), lax.axis_index("emp")
    left, right = device(x + 3, y, c, z), device(x + 1, y, c, z)
    down, up = device(x, y + 3, c, z), device(x, y + 1, c, z)
    back, ahead = (w, lax.rem(z + 12, 16)), (w, lax.rem(z + 4, 16))
    twin = (w + 1 - 2 * c, z)

    barrier = pltpu.get_barrier_semaphore()

    def greet_z(d, _):
        pl.semaphore_signal(barrier, inc=1, device_id=(w, lax.rem(z + d, 16)), device_id_type=MESH)
        return 0

    def greet_w(d, _):
        pl.semaphore_signal(barrier, inc=1, device_id=(lax.rem(w + d, 32), z), device_id_type=MESH)
        return 0

    lax.fori_loop(1, 16, greet_z, 0)
    lax.fori_loop(1, 32, greet_w, 0)
    keep = [
        pltpu.make_async_copy(em, cols.at[a, w], keep_sem.at[0]),
        pltpu.make_async_copy(wk, rows.at[b], keep_sem.at[1]),
    ]
    for one in keep:
        one.start()
    small_all[a] = small[...]
    pl.semaphore_wait(barrier, 46)

    remote(em, cols.at[a, w], z_send, z_recv.at[0], ahead).start()
    remote(em, cols.at[a, w], z_send, z_recv.at[1], back).start()
    for d in (1, 2, 3):
        remote(
            small, small_all.at[a], small_send, small_recv, (w, lax.rem(z + 4 * d, 16))
        ).start()

    def unit(p, i, j):
        return cols.at[p, (lax.rem(x + i, 4) * 4 + lax.rem(y + j, 4)) * 2 + c]

    def half(ref, k):
        return ref.at[:, :, pl.ds(1024 * k, 1024)]

    def send_own(s, src):
        p = lax.rem(a + s, 4)
        for k, to in enumerate((right, left, up, down)):
            remote(src, cols.at[p, w], xy_send.at[k], xy_recv.at[s, k], to).start()
        remote(src, cols.at[p, w], core_send, core_recv, twin).start()

    def push(src, k, sem):
        to = (right, left, up, down)[k]
        remote(src, src, xy_send.at[k], sem, to).start()

    def relay_first(s):
        p = lax.rem(a + s, 4)
        for k, (i, j) in enumerate(((3, 0), (1, 0), (0, 3), (0, 1))):
            got = unit(p, i, j)
            took(got, xy_recv.at[s, k])
            push(half(got, k % 2), k, xy_recv.at[s, 4 + k // 2])
            if k < 2:
                push(got.at[0], 2, xy_recv.at[s, 6 + k])
                push(got.at[0], 3, xy_recv.at[s, 9 + k])
            else:
                push(got.at[1], 0, xy_recv.at[s, 12 + k - 2])
                push(got.at[1], 1, xy_recv.at[s, 15 + k - 2])

    def core_push(p, i, j):
        got = unit(p, i, j)
        remote(got, got, core_send, core_recv, twin).start()

    def relay_second(s):
        p = lax.rem(a + s, 4)
        got = unit(p, 2, 0)
        took(got, xy_recv.at[s, 4])
        push(got.at[0], 2, xy_recv.at[s, 8])
        push(got.at[0], 3, xy_recv.at[s, 11])
        got = unit(p, 0, 2)
        took(got, xy_recv.at[s, 5])
        push(got.at[1], 0, xy_recv.at[s, 14])
        push(got.at[1], 1, xy_recv.at[s, 17])
        for i, j in ((3, 0), (1, 0), (0, 3), (0, 1), (2, 0), (0, 2)):
            core_push(p, i, j)

    def relay_third(s, ms):
        p = lax.rem(a + s, 4)
        for m in ms:
            o = (3, 1, 2)[m]
            for k, (g, i, j) in enumerate(((0, o, 3), (0, o, 1), (1, 3, o), (1, 1, o))):
                got = unit(p, i, j).at[g]
                took(got, xy_recv.at[s, 6 + 3 * k + m])
                part = got.at[:, pl.ds(1024 * (k % 2), 1024)]
                push(part, (2, 3, 0, 1)[k], xy_recv.at[s, 18])

    def finish(s):
        p = lax.rem(a + s, 4)
        took(cols.at[p, pl.ds(0, 3)], xy_recv.at[s, 18])
        for i in (1, 2, 3):
            for j in (1, 2, 3):
                core_push(p, i, j)

    def row_chunk(block, j):
        return block.at[pl.ds(j * (RW // CHUNKS), RW // CHUNKS)]

    def send_rows():
        for j in range(CHUNKS):
            src = row_chunk(wk, j)

            @pl.when(b < 3)
            def _():
                remote(src, row_chunk(rows.at[b], j), row_send.at[0, 0], row_recv.at[0, 0, j], (w, z + 1)).start()

            @pl.when(b > 0)
            def _():
                remote(src, row_chunk(rows.at[b], j), row_send.at[1, 0], row_recv.at[1, 0, j], (w, z - 1)).start()

    def relay_rows(d):
        for j in range(CHUNKS):

            @pl.when(b >= d)
            def _():
                took(row_chunk(rows.at[b - d], j), row_recv.at[0, d - 1, j])

            if d < 3:

                @pl.when((b >= d) & (b < 3))
                def _():
                    got = row_chunk(rows.at[b - d], j)
                    remote(got, got, row_send.at[0, d], row_recv.at[0, d, j], (w, z + 1)).start()

            @pl.when(b + d <= 3)
            def _():
                took(row_chunk(rows.at[b + d], j), row_recv.at[1, d - 1, j])

            if d < 3:

                @pl.when((b + d <= 3) & (b > 0))
                def _():
                    got = row_chunk(rows.at[b + d], j)
                    remote(got, got, row_send.at[1, d], row_recv.at[1, d, j], (w, z - 1)).start()

    send_own(0, em)
    relay_first(0)
    relay_second(0)
    send_rows()
    relay_third(0, (0, 1))

    took(small_all.at[pl.ds(0, 3)], small_recv)
    flags = small_all[...]
    line = lax.broadcasted_iota(jnp.int32, flags.shape, 1)
    mine = (line >= 8 + 4 * a) & (line < 12 + 4 * a)
    top[0] = jnp.full((8, 128), jnp.sum(jnp.where(mine, flags, 0.0)), jnp.float32)

    def top_to_z(d, _):
        remote(top.at[0], top_z.at[d - 1], top_send.at[0], top_recv.at[0], (w, lax.rem(z + d, 16))).start()
        return 0

    lax.fori_loop(1, 16, top_to_z, 0)
    relay_third(0, (2,))

    got = cols.at[lax.rem(a + 3, 4), w]
    took(got, z_recv.at[0])
    remote(half(got, 0), half(got, 0), z_send, z_recv.at[2], ahead).start()
    send_own(3, got)
    got = cols.at[lax.rem(a + 1, 4), w]
    took(got, z_recv.at[1])
    remote(half(got, 1), half(got, 1), z_send, z_recv.at[2], back).start()
    send_own(1, got)
    finish(0)

    took(top_z.at[pl.ds(0, 15)], top_recv.at[0])
    top[1] = jnp.maximum(top[0], jnp.max(top_z[...], axis=0))

    def top_to_w(d, _):
        remote(top.at[1], top_w.at[d - 1], top_send.at[1], top_recv.at[1], (lax.rem(w + d, 32), z)).start()
        return 0

    lax.fori_loop(1, 32, top_to_w, 0)

    relay_first(3)
    relay_first(1)
    relay_second(3)
    relay_second(1)
    got = cols.at[lax.rem(a + 2, 4), w]
    took(got, z_recv.at[2])
    send_own(2, got)
    relay_rows(1)
    relay_third(3, (0, 1, 2))
    relay_third(1, (0, 1, 2))
    relay_first(2)
    relay_second(2)
    relay_rows(2)
    finish(3)
    finish(1)
    relay_third(2, (0, 1, 2))
    finish(2)
    relay_rows(3)

    took(top_w.at[pl.ds(0, 31)], top_recv.at[1])
    peak_out[...] = jnp.maximum(top[1], jnp.max(top_w[...], axis=0))
    small_out[...] = small_all[...]

    for one in keep:
        one.wait()
    took(cols.at[pl.ds(0, 2)], core_recv)
    took(cols.at[pl.ds(0, 2)], core_send)
    for k in range(4):
        took(cols.at[0, pl.ds(0, 15)], xy_send.at[k])
    took(cols.at[0, pl.ds(0, 3)], z_send)
    took(small_all.at[pl.ds(0, 3)], small_send)
    took(top_z.at[pl.ds(0, 15)], top_send.at[0])
    took(top_w.at[pl.ds(0, 31)], top_send.at[1])
    for d in range(3):

        @pl.when((b >= d) & (b < 3))
        def _():
            took(rows.at[0], row_send.at[0, d])

        @pl.when((b + d <= 3) & (b > 0))
        def _():
            took(rows.at[0], row_send.at[1, d])


def gather(wk, em, small):
    f32 = jnp.float32
    return pl.pallas_call(
        gather_kernel,
        out_shape=[
            jax.ShapeDtypeStruct((4, RW, E), jnp.bfloat16),
            jax.ShapeDtypeStruct((4, 32, 2, 16, 2048), jnp.bfloat16),
            jax.ShapeDtypeStruct((4, 24, 128), f32),
            jax.ShapeDtypeStruct((8, 128), f32),
        ],
        in_specs=[ANY, ANY, VMEM],
        out_specs=[ANY, ANY, VMEM, VMEM],
        scratch_shapes=[
            pltpu.VMEM((4, 24, 128), f32),
            pltpu.VMEM((2, 8, 128), f32),
            pltpu.VMEM((15, 8, 128), f32),
            pltpu.VMEM((31, 8, 128), f32),
            DMA((2,)), DMA, DMA((3,)), DMA((4,)), DMA((4, 19)), DMA, DMA,
            DMA((2, 3)), DMA((2, 3, CHUNKS)), DMA, DMA, DMA((2,)), DMA((2,)),
        ],
        compiler_params=pltpu.CompilerParams(collective_id=0, has_side_effects=True),
        name="gather",
    )(wk, em, small)


def build_kernel(row_s, plane_s, col_s, count_s, row_ref, col_ref, tile_ref):
    t = pl.program_id(0)

    @pl.when(t < count_s[0])
    def _():
        both = col_ref[...].reshape(32, 16, RE).astype(jnp.float32)
        upper = (col_s[t] // 16) == 1
        cols = jnp.where(upper, both[:, 8:, :], both[:, :8, :]).reshape(E, RE)
        inv_cols = lax.rsqrt(jnp.sum(cols * cols, axis=0, keepdims=True) * (1.0 / E) + EPSILON)
        cols = cols.astype(jnp.bfloat16)
        for j in range(4):
            part = row_ref[0, pl.ds(j * 256, 256), :]
            wide = part.astype(jnp.float32)
            inv_rows = lax.rsqrt(jnp.sum(wide * wide, axis=1, keepdims=True) * (1.0 / E) + EPSILON)
            cosine = jnp.dot(part, cols, preferred_element_type=jnp.float32)
            cosine = cosine * inv_rows * inv_cols * (1.0 / E)
            tile_ref[0, pl.ds(j * 256, 256), :] = jnp.exp((cosine - 1.0) * (1.0 / SOFTMAX_TEMP)).astype(jnp.bfloat16)

    @pl.when(t >= count_s[0])
    def _():
        tile_ref[...] = jnp.zeros_like(tile_ref)


def build(slots, row, plane, col, count, rows, cols):
    return pl.pallas_call(
        build_kernel,
        out_shape=jax.ShapeDtypeStruct((slots, RW, RE), jnp.bfloat16),
        grid_spec=pltpu.PrefetchScalarGridSpec(
            num_scalar_prefetch=4,
            grid=(slots,),
            in_specs=[
                pl.BlockSpec((1, RW, E), lambda t, r, p, k, n: (r[t], 0, 0)),
                pl.BlockSpec(
                    (1, 32, 1, 16, RE),
                    lambda t, r, p, k, n: (p[t], 0, lax.rem(k[t] // 8, 2), 0, lax.rem(k[t], 8)),
                ),
            ],
            out_specs=pl.BlockSpec((1, RW, RE), lambda t, r, p, k, n: (t, 0, 0)),
        ),
        compiler_params=pltpu.CompilerParams(dimension_semantics=("arbitrary",)),
        name="build_tiles",
    )(row, plane, col, count, rows, cols)


def pick(block, line):
    at = lax.broadcasted_iota(jnp.int32, block.shape, 0)
    first = jnp.sum(jnp.where(at == 2 * line, block, 0.0), axis=0, keepdims=True)
    second = jnp.sum(jnp.where(at == 2 * line + 1, block, 0.0), axis=0, keepdims=True)
    return jnp.concatenate([first, second], axis=1)


def in_two(vector):
    wide = jnp.broadcast_to(vector, (16, vector.shape[1]))
    high = wide.astype(jnp.bfloat16).astype(jnp.float32)
    at = lax.broadcasted_iota(jnp.int32, wide.shape, 0)
    return jnp.where(at == 0, high, jnp.where(at == 1, wide - high, 0.0)).astype(jnp.bfloat16)


def iterate_kernel(
    slots,
    row_s, plane_s, col_s, tiles, spots, worker_mass, employer_mass,
    worker_out, employer_out,
    row_buf, part, col_own, col_buf, plane_buf, scale_buf, out_buf,
    row_send, row_recv, col_send, col_recv, plane_send, plane_recv,
    scale_send, scale_recv, out_send, out_recv,
):
    x, y, c, a, b = place()
    w, z = lax.axis_index("wrk"), lax.axis_index("emp")
    barrier = pltpu.get_barrier_semaphore()

    def greet_w(d, _):
        pl.semaphore_signal(barrier, inc=1, device_id=(lax.rem(w + d, 32), z), device_id_type=MESH)
        return 0

    lax.fori_loop(1, 32, greet_w, 0)
    for d in (1, 2, 3):
        pl.semaphore_signal(barrier, inc=1, device_id=(w, lax.rem(z + 4 * d, 16)), device_id_type=MESH)
        pl.semaphore_signal(barrier, inc=1, device_id=(w, 4 * a + lax.rem(b + d, 4)), device_id_type=MESH)

    row_line = lax.broadcasted_iota(jnp.int32, (8, 512), 0)
    spot = lax.broadcasted_iota(jnp.int32, (256, slots), 0)

    for it in range(ITERS):

        def row_step(t, total):
            if it == 0:
                scale = jnp.ones((1, RE), jnp.float32)
            else:
                scale = pick(scale_buf[it - 1, col_s[t]], plane_s[t])
            sums = lax.dot_general(
                in_two(scale), tiles[t], (((1,), (1,)), ((), ())), preferred_element_type=jnp.float32
            )
            sums = sums[0:1] + sums[1:2]
            line = 2 * row_s[t]
            total = total + jnp.where(row_line == line, sums[:, :512], 0.0)
            return total + jnp.where(row_line == line + 1, sums[:, 512:], 0.0)

        row_buf[it, b] = lax.fori_loop(0, slots, row_step, jnp.zeros((8, 512), jnp.float32))
        if it == 0:
            pl.semaphore_wait(barrier, 37)
        for d in (1, 2, 3):
            mine = row_buf.at[it, b]
            remote(mine, mine, row_send.at[it], row_recv.at[it], (w, 4 * a + lax.rem(b + d, 4))).start()
        took(row_buf.at[it, pl.ds(0, 3)], row_recv.at[it])
        row_total = (row_buf[it, 0] + row_buf[it, 1]) + (row_buf[it, 2] + row_buf[it, 3])
        worker_scale = worker_mass[a] / row_total
        if it == ITERS - 1:
            out_buf[a] = SOFTMAX_TEMP * jnp.log(worker_scale)
            for d in (1, 2, 3):
                remote(out_buf.at[a], out_buf.at[a], out_send, out_recv, (w, lax.rem(z + 4 * d, 16))).start()

        def col_step(t, _):
            scale = pick(worker_scale, row_s[t])
            sums = jnp.dot(in_two(scale), tiles[t], preferred_element_type=jnp.float32)
            part[t] = sums[0:1] + sums[1:2]
            return 0

        lax.fori_loop(0, slots, col_step, 0)
        sums = part[...].reshape(slots, RE)
        totals = jnp.dot(
            jnp.where(spot == spots[0:1, :slots], 1.0, 0.0), sums[:, :128],
            precision=lax.Precision.HIGHEST, preferred_element_type=jnp.float32,
        ) + jnp.dot(
            jnp.where(spot == spots[0:1, :slots] + 1, 1.0, 0.0), sums[:, 128:],
            precision=lax.Precision.HIGHEST, preferred_element_type=jnp.float32,
        )
        col_own[it] = totals.reshape(32, 8, 128)

        def scatter(d, _):
            to = lax.rem(w + d, 32)
            remote(col_own.at[it, to], col_buf.at[it, d - 1], col_send.at[it], col_recv.at[it], (to, z)).start()
            return 0

        lax.fori_loop(1, 32, scatter, 0)
        took(col_buf.at[it], col_recv.at[it])
        plane_buf[it, a] = col_own[it, w] + jnp.sum(col_buf[it], axis=0)
        for d in (1, 2, 3):
            mine = plane_buf.at[it, a]
            remote(mine, mine, plane_send.at[it], plane_recv.at[it], (w, lax.rem(z + 4 * d, 16))).start()
        took(plane_buf.at[it, pl.ds(0, 3)], plane_recv.at[it])
        column_total = (plane_buf[it, 0] + plane_buf[it, 1]) + (plane_buf[it, 2] + plane_buf[it, 3])
        scale_buf[it, w] = employer_mass[...] / column_total

        def share(d, _):
            mine = scale_buf.at[it, w]
            remote(mine, mine, scale_send.at[it], scale_recv.at[it], (lax.rem(w + d, 32), z)).start()
            return 0

        lax.fori_loop(1, 32, share, 0)
        took(scale_buf.at[it, pl.ds(0, 31)], scale_recv.at[it])

    employer_out[...] = SOFTMAX_TEMP * jnp.log(scale_buf[ITERS - 1])
    took(out_buf.at[pl.ds(0, 3)], out_recv)
    worker_out[...] = out_buf[...]

    took(out_buf.at[pl.ds(0, 3)], out_send)
    for it in range(ITERS):
        took(row_buf.at[it, pl.ds(0, 3)], row_send.at[it])
        took(col_buf.at[it], col_send.at[it])
        took(plane_buf.at[it, pl.ds(0, 3)], plane_send.at[it])
        took(scale_buf.at[it, pl.ds(0, 31)], scale_send.at[it])


def iterate(slots, cid, row, plane, col, tiles, spots, worker_mass, employer_mass):
    f32 = jnp.float32
    return pl.pallas_call(
        functools.partial(iterate_kernel, slots),
        out_shape=[jax.ShapeDtypeStruct((4, 8, 512), f32), jax.ShapeDtypeStruct((32, 8, 128), f32)],
        in_specs=[SMEM, SMEM, SMEM, VMEM, VMEM, VMEM, VMEM],
        out_specs=[VMEM, VMEM],
        scratch_shapes=[
            pltpu.VMEM((ITERS, 4, 8, 512), f32),
            pltpu.VMEM((slots, 1, RE), f32),
            pltpu.VMEM((ITERS, 32, 8, 128), f32),
            pltpu.VMEM((ITERS, 31, 8, 128), f32),
            pltpu.VMEM((ITERS, 4, 8, 128), f32),
            pltpu.VMEM((ITERS, 32, 8, 128), f32),
            pltpu.VMEM((4, 8, 512), f32),
        ]
        + [DMA((ITERS,))] * 8
        + [DMA, DMA],
        compiler_params=pltpu.CompilerParams(
            collective_id=cid, has_side_effects=True, vmem_limit_bytes=44 << 20
        ),
        name=f"iterate_{slots}",
    )(row, plane, col, tiles, spots, worker_mass, employer_mass)


def shards(worker_emb, employer_emb, eligible, worker_mass, employer_mass):
    a = lax.axis_index("emp") // 4
    w = lax.axis_index("wrk")
    em = employer_emb.reshape(8, 2, 2, 2048).transpose(2, 1, 0, 3).reshape(2, 16, 2048)
    mass = lax.dynamic_slice_in_dim(employer_mass, w * RE, RE, 0).reshape(2, 128)
    small = jnp.concatenate(
        [
            jnp.pad(mass, ((0, 6), (0, 0))),
            jnp.pad(eligible.astype(jnp.float32), ((0, 0), (0, 96))),
        ],
        axis=0,
    )
    rows, cols, small_all, peak = gather(worker_emb, em, small)

    flags = lax.dynamic_slice_in_dim(small_all[:, 8:, :32], 4 * a, 4, 1).reshape(512)
    order = jnp.cumsum(flags.astype(jnp.int32))
    count = order[511:]
    most = SLOTS[-1]
    slot = jnp.minimum(jnp.arange(most, dtype=jnp.int32), jnp.maximum(count[0] - 1, 0))
    index = jnp.minimum(jnp.sum((order[None, :] <= slot[:, None]).astype(jnp.int32), axis=1), 511)
    plane, row, col = index // 128, index // 32 % 4, index % 32
    spots = jnp.broadcast_to((col * 8 + plane * 2)[None, :], (8, most))
    masses = small_all[:, :2, :].reshape(8, 128)

    def run(slots, cid):
        def branch():
            tiles = build(slots, row, plane, col, count, rows, cols)
            return iterate(
                slots, cid, row, plane, col, tiles, spots, worker_mass.reshape(4, 8, 512), masses
            )

        return branch

    worker_pot, employer_pot = lax.cond(peak[0, 0] <= SLOTS[0], run(SLOTS[0], 1), run(SLOTS[1], 2))
    employer_pot = lax.dynamic_slice_in_dim(employer_pot, 2 * a, 2, 1)
    return worker_pot.reshape(-1), employer_pot.reshape(-1)


def solution(mesh):
    return jax.shard_map(
        shards,
        mesh=mesh,
        in_specs=(P(("wrk", "emp"), None), P("wrk", "emp"), P("wrk", "emp"), P("wrk"), P("emp")),
        out_specs=(P("wrk"), P("emp")),
        check_vma=False,
    )
```

```python
import functools

import jax
import jax.numpy as jnp
from jax import lax
from jax.experimental import pallas as pl
from jax.experimental.pallas import tpu as pltpu
from jax.sharding import PartitionSpec as P

E = 256
ITERS = 3
SOFTMAX_TEMP = 0.25
EPSILON = 1e-06
RW = 1024
RE = 256
SLOTS = (13, 17, 48)
CHUNKS = 4
ORDER = (
    "Z", "o0", "o1", "f00", "f01", "f02", "f03", "f10", "f11", "f12", "f13", "s00", "s01", "R", "s10", "s11",
    "o2", "o3", "t00", "t01", "t02", "t03", "t10", "t11", "t12", "t13", "f20", "f21", "f22", "f23", "f30", "o4",
    "o5", "f31", "f32", "f33", "r10", "e0", "s21", "s20", "e1", "r11", "f40", "f41", "f42", "f43", "f51", "s30",
    "s31", "f50", "f52", "f53", "r12", "t20", "t21", "t22", "t23", "s40", "s41", "r13", "t30", "t31", "t32",
    "t33", "s50", "s51", "e2", "t40", "t41", "t42", "t43", "o6", "o7", "m0", "r20", "e3", "t50", "t51", "t52",
    "t53", "r21", "m1", "e4", "f60", "f61", "f62", "f63", "f70", "f71", "f72", "f73", "r22", "e5", "s60", "s61",
    "m2", "s70", "s71", "r23", "m3", "r30", "t60", "t61", "t62", "t63", "r31", "m4", "t70", "t71", "t72", "t73",
    "e6", "r32", "m5", "e7", "r33", "m6", "m7",
)
MESH = pl.DeviceIdType.MESH
VMEM = pl.BlockSpec(memory_space=pltpu.VMEM)
SMEM = pl.BlockSpec(memory_space=pltpu.SMEM)
HBM = pl.BlockSpec(memory_space=pltpu.HBM)
DMA = pltpu.SemaphoreType.DMA


def place():
    w, z = lax.axis_index("wrk"), lax.axis_index("emp")
    return w // 8, lax.rem(w // 2, 4), lax.rem(w, 2), z // 4, lax.rem(z, 4)


def device(x, y, c, z):
    return ((lax.rem(x, 4) * 4 + lax.rem(y, 4)) * 2 + c, lax.rem(z, 16))


def remote(src, dst, send, recv, to):
    return pltpu.make_async_remote_copy(
        src_ref=src, dst_ref=dst, send_sem=send, recv_sem=recv, device_id=to, device_id_type=MESH
    )


def took(ref, sem):
    pltpu.make_async_copy(ref, ref, sem).wait()


def gather_kernel(
    wk, em_all, eligible_all, mass_all,
    rows, cols, lists, spots, masses, peak,
    em, eligible, mass, shard, small_all, top, top_all,
    load_sem, keep_sem, z_send, z_recv, xy_send, xy_recv, core_send, core_recv,
    row_send, row_recv, small_send, small_recv, top_send, top_recv,
):
    x, y, c, a, b = place()
    w, z = lax.axis_index("wrk"), lax.axis_index("emp")
    left, right = device(x + 3, y, c, z), device(x + 1, y, c, z)
    down, up = device(x, y + 3, c, z), device(x, y + 1, c, z)
    back, ahead = (w, lax.rem(z + 12, 16)), (w, lax.rem(z + 4, 16))
    twin = (w + 1 - 2 * c, z)

    loads = [
        pltpu.make_async_copy(src, dst, load_sem.at[k])
        for k, (src, dst) in enumerate(((em_all, em), (eligible_all, eligible), (mass_all, mass)))
    ]
    for one in loads:
        one.start()
    top_all[...] = jnp.zeros_like(top_all)
    barrier = pltpu.get_barrier_semaphore()
    beside = [(w, 4 * a + lax.rem(b + d, 4)) for d in (1, 3)]
    for to in (left, right, down, up, back, ahead, twin, *beside):
        pl.semaphore_signal(barrier, inc=1, device_id=to, device_id_type=MESH)

    for one in loads:
        one.wait()
    for k in range(2):
        for g in range(2):
            at = 2048 * g + 1024 * k
            for q in range(4):
                here = at + RE * q
                shard[k, g, q] = jnp.concatenate(
                    [em[:, here : here + RE], em[:, 4096 + here : 4096 + here + RE]], axis=0
                )
    small_all[a] = jnp.zeros((24, 128), jnp.float32)
    small_all[a, 0:2, :] = mass[pl.ds(2 * w, 2), :]
    small_all[a, 8:24, 0:32] = eligible[...].astype(jnp.float32)
    keep = [
        pltpu.make_async_copy(shard, cols.at[a, :, x, y, c], keep_sem.at[0]),
        pltpu.make_async_copy(wk, rows.at[b], keep_sem.at[1]),
    ]
    for one in keep:
        one.start()
    pl.semaphore_wait(barrier, 9)

    xs = [lax.rem(x + i, 4) for i in range(4)]
    ys = [lax.rem(y + i, 4) for i in range(4)]
    ps = [lax.rem(a + i, 4) for i in range(4)]
    near = (right, left, up, down)

    def part(s):
        return cols.at[ps[(0, 0, 3, 1, 3, 1, 2, 2)[s]], (0, 1, 0, 0, 1, 1, 0, 1)[s]]

    def push(src, k, kind, sem):
        remote(src, src, xy_send.at[kind, k], sem, near[k]).start()

    def lanes(ref, k):
        return ref.at[pl.ds(2 * k, 2)] if len(ref.shape) == 3 else ref.at[:, pl.ds(2 * k, 2)]

    def z_own():
        for k in range(2):
            for g, to in enumerate((ahead, back)):
                remote(shard.at[k], cols.at[a, k, x, y, c], z_send, z_recv.at[g, k], to).start()
            if k == 0:
                for g, to in enumerate((ahead, back)):
                    remote(small_all.at[a], small_all.at[a], small_send, small_recv.at[g], to).start()

    def own(s):
        got = part(s).at[x, y, c]
        if 2 <= s < 6:
            g, k = s % 2, s // 4
            took(got, z_recv.at[g, k])
            if g == k:
                remote(got, got, z_send, z_recv.at[2, k], (ahead, back)[g]).start()
            if s == 2:
                few = small_all.at[ps[3]]
                took(few, small_recv.at[0])
                remote(few, few, small_send, small_recv.at[2], ahead).start()
        if s >= 6:
            took(got, z_recv.at[2, s - 6])
        for k in range(4):
            src = shard.at[s, k // 2] if s < 2 else got.at[k // 2]
            remote(src, got.at[k // 2], xy_send.at[0, k], xy_recv.at[s, k], near[k]).start()
        if s == 1:
            keep[0].wait()

    def first(s, k):
        i, j = ((3, 0), (1, 0), (0, 3), (0, 1))[k]
        got = part(s).at[xs[i], ys[j], c, k // 2]
        took(got, xy_recv.at[s, k])
        push(lanes(got, k % 2), k, 1, xy_recv.at[s, 4 + k // 2])

    def second(s, axis):
        took(part(s).at[x, y, c, axis], xy_recv.at[s, 4 + axis])
        line = part(s).at[:, y, c, 0] if axis == 0 else part(s).at[x, :, c, 1]
        for k in range(2):
            push(line, 2 - 2 * axis + k, 2, xy_recv.at[s, 6 + 2 * axis + k])

    def third(s, k):
        line = part(s).at[:, ys[3 - 2 * k], c, 0] if k < 2 else part(s).at[xs[7 - 2 * k], :, c, 1]
        took(line, xy_recv.at[s, 6 + k])
        push(lanes(line, k % 2), (2, 3, 0, 1)[k], 3, xy_recv.at[s, 10 + k // 2])

    def finish(s):
        took(part(s).at[:, y, c, 0], xy_recv.at[s, 10])
        took(part(s).at[:, y, c, 0], xy_recv.at[s, 11])
        got = part(s).at[:, :, c]
        remote(got, got, core_send, core_recv, twin).start()

    def row_chunk(block, j):
        return block.at[pl.ds(j * (RW // CHUNKS), RW // CHUNKS)]

    def send_rows():
        for j in range(CHUNKS):
            src = row_chunk(wk, j)

            @pl.when(b < 3)
            def _():
                remote(src, row_chunk(rows.at[b], j), row_send.at[0, 0], row_recv.at[0, 0, j], (w, z + 1)).start()

            @pl.when(b > 0)
            def _():
                remote(src, row_chunk(rows.at[b], j), row_send.at[1, 0], row_recv.at[1, 0, j], (w, z - 1)).start()

    def relay(d, j):
        @pl.when(b >= d)
        def _():
            took(row_chunk(rows.at[b - d], j), row_recv.at[0, d - 1, j])

        if d < 3:

            @pl.when((b >= d) & (b < 3))
            def _():
                got = row_chunk(rows.at[b - d], j)
                remote(got, got, row_send.at[0, d], row_recv.at[0, d, j], (w, z + 1)).start()

        @pl.when(b + d <= 3)
        def _():
            took(row_chunk(rows.at[b + d], j), row_recv.at[1, d - 1, j])

        if d < 3:

            @pl.when((b + d <= 3) & (b > 0))
            def _():
                got = row_chunk(rows.at[b + d], j)
                remote(got, got, row_send.at[1, d], row_recv.at[1, d, j], (w, z - 1)).start()

    def list_tiles():
        took(small_all.at[0], small_recv.at[1])
        took(small_all.at[0], small_recv.at[2])
        masses[...] = small_all[:, 0:2, :].reshape(8, 128)
        flags = small_all[:, 8:24, :].reshape(64, 128)
        line = lax.broadcasted_iota(jnp.int32, (64, 128), 0)
        lane = lax.broadcasted_iota(jnp.int32, (64, 128), 1)
        group = lax.rem(line, 16) // 4
        most = jnp.zeros((1, 1), jnp.float32)
        for g in range(4):
            most = jnp.maximum(most, jnp.sum(jnp.where(group == g, flags, 0.0), keepdims=True))
        top[0] = jnp.broadcast_to(most, (8, 128))
        mine = jnp.where(group == a, flags, 0.0)
        upto = (
            lax.broadcasted_iota(jnp.int32, (128, 128), 0) <= lax.broadcasted_iota(jnp.int32, (128, 128), 1)
        ).astype(jnp.float32)
        above = (
            lax.broadcasted_iota(jnp.int32, (64, 64), 1) < lax.broadcasted_iota(jnp.int32, (64, 64), 0)
        ).astype(jnp.float32)
        before = jnp.sum(jnp.dot(above, mine, preferred_element_type=jnp.float32), axis=1, keepdims=True)
        order = jnp.dot(mine, upto, preferred_element_type=jnp.float32) + before
        slot = lane.astype(jnp.float32)
        ends = before + jnp.sum(mine, axis=1, keepdims=True)
        slot_line = jnp.sum(jnp.where(ends <= slot, 1.0, 0.0), axis=0, keepdims=True)
        hit = jnp.where(line.astype(jnp.float32) == slot_line, 1.0, 0.0)
        there = lax.dot_general(order, hit, (((0,), (0,)), ((), ())), preferred_element_type=jnp.float32)
        slot_lane = jnp.sum(jnp.where(there <= slot[0:1], 1.0, 0.0), axis=0, keepdims=True)
        count = jnp.sum(mine, keepdims=True)
        codes = jnp.where(slot[0:1] < count, slot_line * 32.0 + slot_lane, 0.0).astype(jnp.int32)
        count = jnp.broadcast_to(count, (1, 128)).astype(jnp.int32)
        plane, row, col = codes // 512, lax.rem(codes // 32, 4), lax.rem(codes, 32)
        at = lax.broadcasted_iota(jnp.int32, (8, 128), 0)
        fields = (
            row, plane, col, count, lax.rem(col // 4, 2), lax.rem(col // 8, 2), lax.rem(col, 4), col // 16,
        )
        table = jnp.zeros((8, 128), jnp.int32)
        for k, field in enumerate(fields):
            table = jnp.where(at == k, field, table)
        lists[...] = table
        spots[...] = jnp.broadcast_to(col * 8 + plane * 2, (8, 128))

    def top_send_to(k, g, to):
        remote(top.at[k], top_all.at[k, g], top_send.at[k, g], top_recv.at[k, g], to).start()

    def maximum(k):
        if k == 0:
            list_tiles()
        else:
            if k <= 4:
                for g in range(2):
                    took(top_all.at[k - 1, g], top_recv.at[k - 1, g])
            else:

                @pl.when(b > 0)
                def _():
                    took(top_all.at[k - 1, 0], top_recv.at[k - 1, 0])

                @pl.when(b < 3)
                def _():
                    took(top_all.at[k - 1, 1], top_recv.at[k - 1, 1])

            top[k] = jnp.maximum(top[k - 1], jnp.maximum(top_all[k - 1, 0], top_all[k - 1, 1]))
        if k < 4:
            for g in range(2):
                top_send_to(k, g, near[2 * (k // 2) + g])
        elif k < 7:

            @pl.when(b < 3)
            def _():
                top_send_to(k, 0, (w, z + 1))

            @pl.when(b > 0)
            def _():
                top_send_to(k, 1, (w, z - 1))

        else:
            top_send_to(k, 0, twin)

    steps = dict(
        m=maximum,
        Z=z_own, o=own, f=first, s=second, t=third, e=finish, R=send_rows, r=relay,
    )
    for step in ORDER:
        steps[step[0]](*map(int, step[1:]))

    took(top_all.at[7, 0], top_recv.at[7, 0])
    peak[...] = jnp.maximum(top[7], top_all[7, 0])

    keep[1].wait()
    took(cols.at[pl.ds(0, 2)], core_recv)
    took(cols.at[pl.ds(0, 2)], core_send)
    for k in range(4):
        took(cols.at[0, 0, 0, pl.ds(0, 2)], xy_send.at[0, k])
        took(cols.at[0, 0, 0, 0], xy_send.at[1, k])
        took(cols.at[0, 0, pl.ds(0, 2)], xy_send.at[2, k])
        took(cols.at[0, 0, 0], xy_send.at[3, k])
    took(cols.at[0, 0, 0, pl.ds(0, 3)], z_send)
    took(small_all.at[pl.ds(0, 3)], small_send)
    for k in range(4):
        for g in range(2):
            took(top.at[k], top_send.at[k, g])
    took(top.at[7], top_send.at[7, 0])
    for k in range(4, 7):

        @pl.when(b < 3)
        def _():
            took(top.at[k], top_send.at[k, 0])

        @pl.when(b > 0)
        def _():
            took(top.at[k], top_send.at[k, 1])

    for d in range(3):

        @pl.when((b >= d) & (b < 3))
        def _():
            took(rows.at[0], row_send.at[0, d])

        @pl.when((b + d <= 3) & (b > 0))
        def _():
            took(rows.at[0], row_send.at[1, d])


def gather(wk, em, eligible, mass):
    f32 = jnp.float32
    return pl.pallas_call(
        gather_kernel,
        out_shape=[
            jax.ShapeDtypeStruct((4, RW, E), jnp.bfloat16),
            jax.ShapeDtypeStruct((4, 2, 4, 4, 2, 2, 4, 16, RE), jnp.bfloat16),
            jax.ShapeDtypeStruct((8, 128), jnp.int32),
            jax.ShapeDtypeStruct((8, 128), jnp.int32),
            jax.ShapeDtypeStruct((8, 128), f32),
            jax.ShapeDtypeStruct((8, 128), f32),
        ],
        in_specs=[HBM] * 4,
        out_specs=[VMEM] * 6,
        scratch_shapes=[
            pltpu.VMEM((8, 8192), jnp.bfloat16),
            pltpu.VMEM((16, 32), jnp.int32),
            pltpu.VMEM((64, 128), f32),
            pltpu.VMEM((2, 2, 4, 16, RE), jnp.bfloat16),
            pltpu.VMEM((4, 24, 128), f32),
            pltpu.VMEM((8, 8, 128), f32),
            pltpu.VMEM((8, 2, 8, 128), f32),
            DMA((3,)), DMA((2,)), DMA, DMA((3, 2)), DMA((4, 4)), DMA((8, 12)), DMA, DMA,
            DMA((2, 3)), DMA((2, 3, CHUNKS)), DMA, DMA((3,)), DMA((8, 2)), DMA((8, 2)),
        ],
        compiler_params=pltpu.CompilerParams(collective_id=0, has_side_effects=True, vmem_limit_bytes=24 << 20),
        name="gather",
    )(wk, em, eligible, mass)


def build_tile(t, lists, rows, cols, tiles):
    row = lists[0, t]
    keep = jnp.where(jnp.full((1, RE), lists[3, t], jnp.int32) > t, 1.0, 0.0)
    both = cols[lists[1, t], lists[4, t], :, :, :, lists[5, t], lists[6, t], :, :]
    both = both.reshape(32, 16, RE).astype(jnp.float32)
    upper = jnp.full((32, 8, RE), lists[7, t], jnp.int32) == 1
    side = jnp.where(upper, both[:, 8:, :], both[:, :8, :]).reshape(E, RE)
    inv_cols = lax.rsqrt(jnp.sum(side * side, axis=0, keepdims=True) * (1.0 / E) + EPSILON)
    inv_cols = inv_cols * (1.0 / E)
    side = side.astype(jnp.bfloat16)
    for j in range(RW // 256):
        part = rows[row, pl.ds(j * 256, 256), :]
        wide = part.astype(jnp.float32)
        inv_rows = lax.rsqrt(jnp.sum(wide * wide, axis=1, keepdims=True) * (1.0 / E) + EPSILON)
        cosine = jnp.dot(part, side, preferred_element_type=jnp.float32) * inv_rows * inv_cols
        value = jnp.exp((cosine - 1.0) * (1.0 / SOFTMAX_TEMP)) * keep
        tiles[t, pl.ds(j * 256, 256), :] = value.astype(jnp.bfloat16)


def in_line(block, lines):
    return jnp.concatenate([jnp.broadcast_to(block[k : k + 1], (16, 128)) for k in lines], axis=1)


def stacked(vector):
    at = lax.broadcasted_iota(jnp.int32, (8, 128), 0)
    out = jnp.zeros((8, 128), jnp.float32)
    for k in range(8):
        out = jnp.where(at == k, vector[:, 128 * k : 128 * k + 128], out)
    return out


def in_two(wide):
    high = wide.astype(jnp.bfloat16).astype(jnp.float32)
    at = lax.broadcasted_iota(jnp.int32, wide.shape, 0)
    return jnp.where(at == 0, high, jnp.where(at == 1, wide - high, 0.0)).astype(jnp.bfloat16)


def iterate_kernel(
    slots,
    lists, rows, cols, spots, worker_mass, employer_mass,
    worker_out, employer_out,
    tiles, row_buf, worker_scale, part, col_own, col_buf, plane_buf, scale_buf, out_buf,
    row_send, row_recv, col_send, col_recv, plane_send, plane_recv,
    scale_send, scale_recv, out_send, out_recv,
):
    x, y, c, a, b = place()
    w, z = lax.axis_index("wrk"), lax.axis_index("emp")
    barrier = pltpu.get_barrier_semaphore()

    def greet_w(d, _):
        pl.semaphore_signal(barrier, inc=1, device_id=(lax.rem(w + d, 32), z), device_id_type=MESH)
        return 0

    lax.fori_loop(1, 32, greet_w, 0)
    for d in (1, 2, 3):
        pl.semaphore_signal(barrier, inc=1, device_id=(w, lax.rem(z + 4 * d, 16)), device_id_type=MESH)
        pl.semaphore_signal(barrier, inc=1, device_id=(w, 4 * a + lax.rem(b + d, 4)), device_id_type=MESH)

    def build_step(t, _):
        build_tile(t, lists, rows, cols, tiles)
        return 0

    lax.fori_loop(0, slots, build_step, 0)
    unroll = slots if slots <= 20 else 4
    spot = lax.broadcasted_iota(jnp.int32, (256, slots), 0)
    block_line = lax.broadcasted_iota(jnp.int32, (8, 128), 0)

    for it in range(ITERS):

        def row_step(t, totals):
            if it == 0:
                scale = jnp.ones((16, RE), jnp.float32)
            else:
                block = scale_buf[it - 1, lists[2, t]]
                line = 2 * lists[1, t]
                first = jnp.sum(jnp.where(block_line == line, block, 0.0), axis=0, keepdims=True)
                second = jnp.sum(jnp.where(block_line == line + 1, block, 0.0), axis=0, keepdims=True)
                scale = jnp.broadcast_to(jnp.concatenate([first, second], axis=1), (16, RE))
            sums = lax.dot_general(
                in_two(scale), tiles[t], (((1,), (1,)), ((), ())), preferred_element_type=jnp.float32
            )
            sums = stacked(sums[0:1] + sums[1:2])
            row = jnp.full((8, 128), lists[0, t], jnp.int32)
            return tuple(total + jnp.where(row == r, sums, 0.0) for r, total in enumerate(totals))

        totals = lax.fori_loop(0, slots, row_step, (jnp.zeros((8, 128), jnp.float32),) * 4, unroll=unroll)
        for r in range(4):
            row_buf[it, b, r] = totals[r]
        if it == 0:
            pl.semaphore_wait(barrier, 37)
        for d in (1, 2, 3):
            mine = row_buf.at[it, b]
            remote(mine, mine, row_send.at[it], row_recv.at[it], (w, 4 * a + lax.rem(b + d, 4))).start()
        took(row_buf.at[it, pl.ds(0, 3)], row_recv.at[it])
        row_total = (row_buf[it, 0] + row_buf[it, 1]) + (row_buf[it, 2] + row_buf[it, 3])
        mass = worker_mass[pl.ds(pl.multiple_of(32 * a, 32), 32), :].reshape(4, 8, 128)
        worker_scale[it] = mass / row_total
        if it == ITERS - 1:
            out_buf[a] = SOFTMAX_TEMP * jnp.log(worker_scale[it])
            for d in (1, 2, 3):
                remote(out_buf.at[a], out_buf.at[a], out_send, out_recv, (w, lax.rem(z + 4 * d, 16))).start()

        def col_step(t, _):
            scale = in_line(worker_scale[it, lists[0, t]], range(8))
            sums = jnp.dot(in_two(scale), tiles[t], preferred_element_type=jnp.float32)
            part[t] = sums[0:1] + sums[1:2]
            return 0

        lax.fori_loop(0, slots, col_step, 0, unroll=unroll)
        sums = part[...].reshape(slots, RE)
        totals = jnp.dot(
            jnp.where(spot == spots[0:1, :slots], 1.0, 0.0), sums[:, :128],
            precision=lax.Precision.HIGHEST, preferred_element_type=jnp.float32,
        ) + jnp.dot(
            jnp.where(spot == spots[0:1, :slots] + 1, 1.0, 0.0), sums[:, 128:],
            precision=lax.Precision.HIGHEST, preferred_element_type=jnp.float32,
        )
        col_own[it] = totals.reshape(32, 8, 128)

        def scatter(d, _):
            to = lax.rem(w + d, 32)
            remote(col_own.at[it, to], col_buf.at[it, d - 1], col_send.at[it], col_recv.at[it], (to, z)).start()
            return 0

        lax.fori_loop(1, 32, scatter, 0)
        took(col_buf.at[it], col_recv.at[it])
        plane_buf[it, a] = col_own[it, w] + jnp.sum(col_buf[it], axis=0)
        for d in (1, 2, 3):
            mine = plane_buf.at[it, a]
            remote(mine, mine, plane_send.at[it], plane_recv.at[it], (w, lax.rem(z + 4 * d, 16))).start()
        took(plane_buf.at[it, pl.ds(0, 3)], plane_recv.at[it])
        column_total = (plane_buf[it, 0] + plane_buf[it, 1]) + (plane_buf[it, 2] + plane_buf[it, 3])
        scale_buf[it, w] = employer_mass[...] / column_total

        def share(d, _):
            mine = scale_buf.at[it, w]
            remote(mine, mine, scale_send.at[it], scale_recv.at[it], (lax.rem(w + d, 32), z)).start()
            return 0

        lax.fori_loop(1, 32, share, 0)
        took(scale_buf.at[it, pl.ds(0, 31)], scale_recv.at[it])

    for k in range(32):
        employer_out[2 * k : 2 * k + 2, :] = SOFTMAX_TEMP * jnp.log(scale_buf[ITERS - 1, k, pl.ds(2 * a, 2), :])
    took(out_buf.at[pl.ds(0, 3)], out_recv)
    worker_out[...] = out_buf[...].reshape(128, 128)

    took(out_buf.at[pl.ds(0, 3)], out_send)
    for it in range(ITERS):
        took(row_buf.at[it, pl.ds(0, 3)], row_send.at[it])
        took(col_buf.at[it], col_send.at[it])
        took(plane_buf.at[it, pl.ds(0, 3)], plane_send.at[it])
        took(scale_buf.at[it, pl.ds(0, 31)], scale_send.at[it])


def iterate(slots, cid, lists, rows, cols, spots, worker_mass, employer_mass):
    f32 = jnp.float32
    return pl.pallas_call(
        functools.partial(iterate_kernel, slots),
        out_shape=[jax.ShapeDtypeStruct((128, 128), f32), jax.ShapeDtypeStruct((64, 128), f32)],
        in_specs=[SMEM] + [VMEM] * 5,
        out_specs=[VMEM, VMEM],
        scratch_shapes=[
            pltpu.VMEM((slots, RW, RE), jnp.bfloat16),
            pltpu.VMEM((ITERS, 4, 4, 8, 128), f32),
            pltpu.VMEM((ITERS, 4, 8, 128), f32),
            pltpu.VMEM((slots, 1, RE), f32),
            pltpu.VMEM((ITERS, 32, 8, 128), f32),
            pltpu.VMEM((ITERS, 31, 8, 128), f32),
            pltpu.VMEM((ITERS, 4, 8, 128), f32),
            pltpu.VMEM((ITERS, 32, 8, 128), f32),
            pltpu.VMEM((4, 4, 8, 128), f32),
        ]
        + [DMA((ITERS,))] * 8
        + [DMA, DMA],
        compiler_params=pltpu.CompilerParams(
            collective_id=cid, has_side_effects=True, vmem_limit_bytes=(20 + slots // 2) << 20
        ),
        name=f"iterate_{slots}",
    )(lists, rows, cols, spots, worker_mass, employer_mass)


def shards(worker_emb, employer_emb, eligible, worker_mass, employer_mass):
    inputs = worker_emb, employer_emb, eligible, employer_mass.reshape(64, 128)
    inputs = [pltpu.with_memory_space_constraint(one, pltpu.HBM) for one in inputs]
    rows, cols, lists, spots, masses, peak = gather(*inputs)
    worker_mass = worker_mass.reshape(128, 128)

    def run(slots, cid):
        return lambda: iterate(slots, cid, lists, rows, cols, spots, worker_mass, masses)

    which = sum((peak[0, 0] > slots).astype(jnp.int32) for slots in SLOTS[:-1])
    worker_pot, employer_pot = lax.switch(which, [run(slots, k + 1) for k, slots in enumerate(SLOTS)])
    return worker_pot.reshape(-1), employer_pot.reshape(-1)


def solution(mesh):
    return jax.shard_map(
        shards,
        mesh=mesh,
        in_specs=(P(("wrk", "emp"), None), P("wrk", "emp"), P("wrk", "emp"), P("wrk"), P("emp")),
        out_specs=(P("wrk"), P("emp")),
        check_vma=False,
    )
```

```python
import functools

import jax
import jax.numpy as jnp
from jax import lax
from jax.experimental import pallas as pl
from jax.experimental.pallas import tpu as pltpu
from jax.sharding import PartitionSpec as P

E = 256
ITERS = 3
SOFTMAX_TEMP = 0.25
EPSILON = 1e-06
RW = 1024
RE = 256
SLOTS = (13, 17, 48)
CHUNKS = 4
ORDER = (
    "Z", "o0", "o1", "f00", "f01", "f02", "f03", "f10", "f11", "f12", "f13", "s00", "s01", "R", "s10", "s11",
    "n", "o2", "o3", "t00", "t01", "t02", "t03", "t10", "t11", "t12", "t13", "f20", "f21", "f22", "f23", "f30",
    "o4", "o5", "f31", "f32", "f33", "r10", "e0", "s21", "s20", "e1", "r11", "f40", "f41", "f42", "f43", "f51",
    "s30", "s31", "f50", "f52", "f53", "r12", "t20", "t21", "t22", "t23", "s40", "s41", "r13", "m0", "t30",
    "t31", "t32", "t33", "s50", "s51", "e2", "t40", "t41", "t42", "t43", "o6", "o7", "e3", "m1", "r20", "t50",
    "t51", "t52", "t53", "r21", "e4", "f60", "f61", "f62", "f63", "f70", "f71", "f72", "f73", "r22", "m2",
    "s60", "s61", "e5", "s70", "s71", "r23", "r30", "t60", "t61", "t62", "t63", "m3", "r31", "t70", "t71",
    "t72", "t73", "e6", "r32", "e7", "r33",
)
MESH = pl.DeviceIdType.MESH
VMEM = pl.BlockSpec(memory_space=pltpu.VMEM)
SMEM = pl.BlockSpec(memory_space=pltpu.SMEM)
HBM = pl.BlockSpec(memory_space=pltpu.HBM)
DMA = pltpu.SemaphoreType.DMA


def place():
    w, z = lax.axis_index("wrk"), lax.axis_index("emp")
    return w // 8, lax.rem(w // 2, 4), lax.rem(w, 2), z // 4, lax.rem(z, 4)


def device(x, y, c, z):
    return ((lax.rem(x, 4) * 4 + lax.rem(y, 4)) * 2 + c, lax.rem(z, 16))


def remote(src, dst, send, recv, to):
    return pltpu.make_async_remote_copy(
        src_ref=src, dst_ref=dst, send_sem=send, recv_sem=recv, device_id=to, device_id_type=MESH
    )


def took(ref, sem):
    pltpu.make_async_copy(ref, ref, sem).wait()


def gather_kernel(
    wk, em_all, eligible_all, mass_all,
    rows, cols, lists, spots, masses, which,
    em, eligible, mass, shard, small_all, top, top_all,
    load_sem, keep_sem, z_send, z_recv, xy_send, xy_recv, core_send, core_recv,
    row_send, row_recv, small_send, small_recv, top_send, top_recv,
):
    x, y, c, a, b = place()
    w, z = lax.axis_index("wrk"), lax.axis_index("emp")
    left, right = device(x + 3, y, c, z), device(x + 1, y, c, z)
    down, up = device(x, y + 3, c, z), device(x, y + 1, c, z)
    back, ahead = (w, lax.rem(z + 12, 16)), (w, lax.rem(z + 4, 16))
    twin = (w + 1 - 2 * c, z)

    loads = [
        pltpu.make_async_copy(src, dst, load_sem.at[k])
        for k, (src, dst) in enumerate(((em_all, em), (eligible_all, eligible), (mass_all, mass)))
    ]
    for one in loads:
        one.start()
    barrier = pltpu.get_barrier_semaphore()
    group = [(w, 4 * a + lax.rem(b + d, 4)) for d in (1, 2, 3)]
    far = [device(x + 2, y, c, z), device(x, y + 2, c, z)]
    for to in (left, right, down, up, back, ahead, twin, *group, *far):
        pl.semaphore_signal(barrier, inc=1, device_id=to, device_id_type=MESH)

    for one in loads:
        one.wait()
    for k in range(2):
        for g in range(2):
            at = 2048 * g + 1024 * k
            for q in range(4):
                here = at + RE * q
                shard[k, g, q] = jnp.concatenate(
                    [em[:, here : here + RE], em[:, 4096 + here : 4096 + here + RE]], axis=0
                )
    small_all[a] = jnp.zeros((24, 128), jnp.float32)
    small_all[a, 0:2, :] = mass[pl.ds(2 * w, 2), :]
    small_all[a, 8:24, 0:32] = eligible[...].astype(jnp.float32)
    keep = [
        pltpu.make_async_copy(shard, cols.at[a, :, x, y, c], keep_sem.at[0]),
        pltpu.make_async_copy(wk, rows.at[b], keep_sem.at[1]),
    ]
    for one in keep:
        one.start()
    pl.semaphore_wait(barrier, 12)

    xs = [lax.rem(x + i, 4) for i in range(4)]
    ys = [lax.rem(y + i, 4) for i in range(4)]
    ps = [lax.rem(a + i, 4) for i in range(4)]
    near = (right, left, up, down)

    def part(s):
        return cols.at[ps[(0, 0, 3, 1, 3, 1, 2, 2)[s]], (0, 1, 0, 0, 1, 1, 0, 1)[s]]

    def push(src, k, kind, sem):
        remote(src, src, xy_send.at[kind, k], sem, near[k]).start()

    def lanes(ref, k):
        return ref.at[pl.ds(2 * k, 2)] if len(ref.shape) == 3 else ref.at[:, pl.ds(2 * k, 2)]

    def z_own():
        for g, to in enumerate((ahead, back)):
            remote(small_all.at[a], small_all.at[a], small_send, small_recv.at[g], to).start()
        for k in range(2):
            for g, to in enumerate((ahead, back)):
                remote(shard.at[k], cols.at[a, k, x, y, c], z_send, z_recv.at[g, k], to).start()

    def relay_small():
        few = small_all.at[ps[3]]
        took(few, small_recv.at[0])
        remote(few, few, small_send, small_recv.at[2], ahead).start()

    def own(s):
        got = part(s).at[x, y, c]
        if 2 <= s < 6:
            g, k = s % 2, s // 4
            took(got, z_recv.at[g, k])
            if g == k:
                remote(got, got, z_send, z_recv.at[2, k], (ahead, back)[g]).start()
        if s >= 6:
            took(got, z_recv.at[2, s - 6])
        for k in range(4):
            src = shard.at[s, k // 2] if s < 2 else got.at[k // 2]
            remote(src, got.at[k // 2], xy_send.at[0, k], xy_recv.at[s, k], near[k]).start()
        if s == 1:
            keep[0].wait()

    def first(s, k):
        i, j = ((3, 0), (1, 0), (0, 3), (0, 1))[k]
        got = part(s).at[xs[i], ys[j], c, k // 2]
        took(got, xy_recv.at[s, k])
        push(lanes(got, k % 2), k, 1, xy_recv.at[s, 4 + k // 2])

    def to_twin(line):
        remote(line, line, core_send, core_recv, twin).start()

    def second(s, axis):
        took(part(s).at[x, y, c, axis], xy_recv.at[s, 4 + axis])
        line = part(s).at[:, y, c, 0] if axis == 0 else part(s).at[x, :, c, 1]
        for k in range(2):
            push(line, 2 - 2 * axis + k, 2, xy_recv.at[s, 6 + 2 * axis + k])
        to_twin(line)

    def third(s, k):
        line = part(s).at[:, ys[3 - 2 * k], c, 0] if k < 2 else part(s).at[xs[7 - 2 * k], :, c, 1]
        took(line, xy_recv.at[s, 6 + k])
        push(lanes(line, k % 2), (2, 3, 0, 1)[k], 3, xy_recv.at[s, 10 + k // 2])
        to_twin(line)

    def finish(s):
        for k, line in enumerate((part(s).at[:, ys[2], c, 0], part(s).at[xs[2], :, c, 1])):
            took(line, xy_recv.at[s, 10 + k])
            to_twin(line)

    def row_chunk(block, j):
        return block.at[pl.ds(j * (RW // CHUNKS), RW // CHUNKS)]

    def send_rows():
        for j in range(CHUNKS):
            src = row_chunk(wk, j)

            @pl.when(b < 3)
            def _():
                remote(src, row_chunk(rows.at[b], j), row_send.at[0, 0], row_recv.at[0, 0, j], (w, z + 1)).start()

            @pl.when(b > 0)
            def _():
                remote(src, row_chunk(rows.at[b], j), row_send.at[1, 0], row_recv.at[1, 0, j], (w, z - 1)).start()

    def relay(d, j):
        @pl.when(b >= d)
        def _():
            took(row_chunk(rows.at[b - d], j), row_recv.at[0, d - 1, j])

        if d < 3:

            @pl.when((b >= d) & (b < 3))
            def _():
                got = row_chunk(rows.at[b - d], j)
                remote(got, got, row_send.at[0, d], row_recv.at[0, d, j], (w, z + 1)).start()

        @pl.when(b + d <= 3)
        def _():
            took(row_chunk(rows.at[b + d], j), row_recv.at[1, d - 1, j])

        if d < 3:

            @pl.when((b + d <= 3) & (b > 0))
            def _():
                got = row_chunk(rows.at[b + d], j)
                remote(got, got, row_send.at[1, d], row_recv.at[1, d, j], (w, z - 1)).start()

    def list_tiles():
        took(small_all.at[0], small_recv.at[1])
        took(small_all.at[0], small_recv.at[2])
        masses[...] = small_all[:, 0:2, :].reshape(8, 128)
        flags = small_all[:, 8:24, :].reshape(64, 128)
        line = lax.broadcasted_iota(jnp.int32, (64, 128), 0)
        lane = lax.broadcasted_iota(jnp.int32, (64, 128), 1)
        group = lax.rem(line, 16) // 4
        most = jnp.zeros((1, 1), jnp.float32)
        for g in range(4):
            most = jnp.maximum(most, jnp.sum(jnp.where(group == g, flags, 0.0), keepdims=True))
        top[0] = jnp.broadcast_to(most, (8, 128))
        mine = jnp.where(group == a, flags, 0.0)
        upto = (
            lax.broadcasted_iota(jnp.int32, (128, 128), 0) <= lax.broadcasted_iota(jnp.int32, (128, 128), 1)
        ).astype(jnp.float32)
        above = (
            lax.broadcasted_iota(jnp.int32, (64, 64), 1) < lax.broadcasted_iota(jnp.int32, (64, 64), 0)
        ).astype(jnp.float32)
        before = jnp.sum(jnp.dot(above, mine, preferred_element_type=jnp.float32), axis=1, keepdims=True)
        order = jnp.dot(mine, upto, preferred_element_type=jnp.float32) + before
        slot = lane.astype(jnp.float32)
        ends = before + jnp.sum(mine, axis=1, keepdims=True)
        slot_line = jnp.sum(jnp.where(ends <= slot, 1.0, 0.0), axis=0, keepdims=True)
        hit = jnp.where(line.astype(jnp.float32) == slot_line, 1.0, 0.0)
        there = lax.dot_general(order, hit, (((0,), (0,)), ((), ())), preferred_element_type=jnp.float32)
        slot_lane = jnp.sum(jnp.where(there <= slot[0:1], 1.0, 0.0), axis=0, keepdims=True)
        count = jnp.sum(mine, keepdims=True)
        codes = jnp.where(slot[0:1] < count, slot_line * 32.0 + slot_lane, 0.0).astype(jnp.int32)
        count = jnp.broadcast_to(count, (1, 128)).astype(jnp.int32)
        plane, row, col = codes // 512, lax.rem(codes // 32, 4), lax.rem(codes, 32)
        at = lax.broadcasted_iota(jnp.int32, (8, 128), 0)
        fields = (
            row, plane, col, count, lax.rem(col // 4, 2), lax.rem(col // 8, 2), lax.rem(col, 4), col // 16,
        )
        table = jnp.zeros((8, 128), jnp.int32)
        for k, field in enumerate(fields):
            table = jnp.where(at == k, field, table)
        lists[...] = table
        spots[...] = jnp.broadcast_to(col * 8 + plane * 2, (8, 128))

    circles = (
        [device(x + d, y, c, z) for d in (1, 2, 3)],
        [device(x, y + d, c, z) for d in (1, 2, 3)],
        group,
        [twin],
    )

    def maximum(k):
        if k == 0:
            list_tiles()
        else:
            for d in range(3):
                took(top_all.at[k - 1, d], top_recv.at[k - 1, d])
            top[k] = jnp.maximum(top[k - 1], jnp.max(top_all[k - 1], axis=0))
        for d, to in enumerate(circles[k]):
            remote(top.at[k], top_all.at[k, d], top_send.at[k, d], top_recv.at[k, d], to).start()

    steps = dict(
        m=maximum, n=relay_small,
        Z=z_own, o=own, f=first, s=second, t=third, e=finish, R=send_rows, r=relay,
    )
    for step in ORDER:
        steps[step[0]](*map(int, step[1:]))

    took(top_all.at[3, 0], top_recv.at[3, 0])
    most = jnp.max(jnp.maximum(top[3], top_all[3, 0]))
    which[0, 0] = sum(jnp.where(most > slots, 1, 0) for slots in SLOTS[:-1]).astype(jnp.int32)

    keep[1].wait()
    took(cols.at[pl.ds(0, 2)], core_recv)
    took(cols.at[pl.ds(0, 2)], core_send)
    for k in range(4):
        took(cols.at[0, 0, 0, pl.ds(0, 2)], xy_send.at[0, k])
        took(cols.at[0, 0, 0, 0], xy_send.at[1, k])
        took(cols.at[0, 0, pl.ds(0, 2)], xy_send.at[2, k])
        took(cols.at[0, 0, 0], xy_send.at[3, k])
    took(cols.at[0, 0, 0, pl.ds(0, 3)], z_send)
    took(small_all.at[pl.ds(0, 3)], small_send)
    for k in range(4):
        for d in range(len(circles[k])):
            took(top.at[k], top_send.at[k, d])

    for d in range(3):

        @pl.when((b >= d) & (b < 3))
        def _():
            took(rows.at[0], row_send.at[0, d])

        @pl.when((b + d <= 3) & (b > 0))
        def _():
            took(rows.at[0], row_send.at[1, d])


def gather(wk, em, eligible, mass):
    f32 = jnp.float32
    return pl.pallas_call(
        gather_kernel,
        out_shape=[
            jax.ShapeDtypeStruct((4, RW, E), jnp.bfloat16),
            jax.ShapeDtypeStruct((4, 2, 4, 4, 2, 2, 4, 16, RE), jnp.bfloat16),
            jax.ShapeDtypeStruct((8, 128), jnp.int32),
            jax.ShapeDtypeStruct((8, 128), jnp.int32),
            jax.ShapeDtypeStruct((8, 128), f32),
            jax.ShapeDtypeStruct((1, 1), jnp.int32),
        ],
        in_specs=[HBM] * 4,
        out_specs=[VMEM] * 5 + [SMEM],
        scratch_shapes=[
            pltpu.VMEM((8, 8192), jnp.bfloat16),
            pltpu.VMEM((16, 32), jnp.int32),
            pltpu.VMEM((64, 128), f32),
            pltpu.VMEM((2, 2, 4, 16, RE), jnp.bfloat16),
            pltpu.VMEM((4, 24, 128), f32),
            pltpu.VMEM((4, 8, 128), f32),
            pltpu.VMEM((4, 3, 8, 128), f32),
            DMA((3,)), DMA((2,)), DMA, DMA((3, 2)), DMA((4, 4)), DMA((8, 12)), DMA, DMA,
            DMA((2, 3)), DMA((2, 3, CHUNKS)), DMA, DMA((3,)), DMA((4, 3)), DMA((4, 3)),
        ],
        compiler_params=pltpu.CompilerParams(collective_id=0, has_side_effects=True, vmem_limit_bytes=24 << 20),
        name="gather",
    )(wk, em, eligible, mass)


def build_tile(t, lists, rows, cols, tiles):
    row = lists[0, t]
    keep = jnp.where(jnp.full((1, RE), lists[3, t], jnp.int32) > t, 1.0, 0.0)
    both = cols[lists[1, t], lists[4, t], :, :, :, lists[5, t], lists[6, t], :, :]
    both = both.reshape(32, 16, RE).astype(jnp.float32)
    upper = jnp.full((32, 8, RE), lists[7, t], jnp.int32) == 1
    side = jnp.where(upper, both[:, 8:, :], both[:, :8, :]).reshape(E, RE)
    inv_cols = lax.rsqrt(jnp.sum(side * side, axis=0, keepdims=True) * (1.0 / E) + EPSILON)
    inv_cols = inv_cols * (1.0 / E)
    side = side.astype(jnp.bfloat16)
    for j in range(RW // 256):
        part = rows[row, pl.ds(j * 256, 256), :]
        wide = part.astype(jnp.float32)
        inv_rows = lax.rsqrt(jnp.sum(wide * wide, axis=1, keepdims=True) * (1.0 / E) + EPSILON)
        cosine = jnp.dot(part, side, preferred_element_type=jnp.float32) * inv_rows * inv_cols
        value = jnp.exp((cosine - 1.0) * (1.0 / SOFTMAX_TEMP)) * keep
        tiles[t, pl.ds(j * 256, 256), :] = value.astype(jnp.bfloat16)


def in_line(block, lines):
    return jnp.concatenate([jnp.broadcast_to(block[k : k + 1], (16, 128)) for k in lines], axis=1)


def stacked(vector):
    at = lax.broadcasted_iota(jnp.int32, (8, 128), 0)
    out = jnp.zeros((8, 128), jnp.float32)
    for k in range(8):
        out = jnp.where(at == k, vector[:, 128 * k : 128 * k + 128], out)
    return out


def in_two(wide):
    high = wide.astype(jnp.bfloat16).astype(jnp.float32)
    at = lax.broadcasted_iota(jnp.int32, wide.shape, 0)
    return jnp.where(at == 0, high, jnp.where(at == 1, wide - high, 0.0)).astype(jnp.bfloat16)


def iterate_kernel(
    slots,
    lists, rows, cols, spots, worker_mass, employer_mass,
    worker_out, employer_out,
    tiles, row_buf, worker_scale, part, col_own, col_buf, plane_buf, scale_buf, out_buf,
    row_send, row_recv, col_send, col_recv, plane_send, plane_recv,
    scale_send, scale_recv, out_send, out_recv,
):
    x, y, c, a, b = place()
    w, z = lax.axis_index("wrk"), lax.axis_index("emp")
    barrier = pltpu.get_barrier_semaphore()

    def greet_w(d, _):
        pl.semaphore_signal(barrier, inc=1, device_id=(lax.rem(w + d, 32), z), device_id_type=MESH)
        return 0

    lax.fori_loop(1, 32, greet_w, 0)
    for d in (1, 2, 3):
        pl.semaphore_signal(barrier, inc=1, device_id=(w, lax.rem(z + 4 * d, 16)), device_id_type=MESH)
        pl.semaphore_signal(barrier, inc=1, device_id=(w, 4 * a + lax.rem(b + d, 4)), device_id_type=MESH)

    def build_step(t, _):
        build_tile(t, lists, rows, cols, tiles)
        return 0

    lax.fori_loop(0, slots, build_step, 0)
    unroll = slots if slots <= 20 else 4
    spot = lax.broadcasted_iota(jnp.int32, (256, slots), 0)
    block_line = lax.broadcasted_iota(jnp.int32, (8, 128), 0)

    for it in range(ITERS):

        def row_step(t, totals):
            if it == 0:
                scale = jnp.ones((16, RE), jnp.float32)
            else:
                block = scale_buf[it - 1, lists[2, t]]
                line = 2 * lists[1, t]
                first = jnp.sum(jnp.where(block_line == line, block, 0.0), axis=0, keepdims=True)
                second = jnp.sum(jnp.where(block_line == line + 1, block, 0.0), axis=0, keepdims=True)
                scale = jnp.broadcast_to(jnp.concatenate([first, second], axis=1), (16, RE))
            sums = lax.dot_general(
                in_two(scale), tiles[t], (((1,), (1,)), ((), ())), preferred_element_type=jnp.float32
            )
            sums = stacked(sums[0:1] + sums[1:2])
            row = jnp.full((8, 128), lists[0, t], jnp.int32)
            return tuple(total + jnp.where(row == r, sums, 0.0) for r, total in enumerate(totals))

        totals = lax.fori_loop(0, slots, row_step, (jnp.zeros((8, 128), jnp.float32),) * 4, unroll=unroll)
        for r in range(4):
            row_buf[it, b, r] = totals[r]
        if it == 0:
            pl.semaphore_wait(barrier, 37)
        for d in (1, 2, 3):
            mine = row_buf.at[it, b]
            remote(mine, mine, row_send.at[it], row_recv.at[it], (w, 4 * a + lax.rem(b + d, 4))).start()
        took(row_buf.at[it, pl.ds(0, 3)], row_recv.at[it])
        row_total = (row_buf[it, 0] + row_buf[it, 1]) + (row_buf[it, 2] + row_buf[it, 3])
        mass = worker_mass[pl.ds(pl.multiple_of(32 * a, 32), 32), :].reshape(4, 8, 128)
        worker_scale[it] = mass / row_total
        if it == ITERS - 1:
            out_buf[a] = SOFTMAX_TEMP * jnp.log(worker_scale[it])
            for d in (1, 2, 3):
                remote(out_buf.at[a], out_buf.at[a], out_send, out_recv, (w, lax.rem(z + 4 * d, 16))).start()

        def col_step(t, _):
            scale = in_line(worker_scale[it, lists[0, t]], range(8))
            sums = jnp.dot(in_two(scale), tiles[t], preferred_element_type=jnp.float32)
            part[t] = sums[0:1] + sums[1:2]
            return 0

        lax.fori_loop(0, slots, col_step, 0, unroll=unroll)
        sums = part[...].reshape(slots, RE)
        totals = jnp.dot(
            jnp.where(spot == spots[0:1, :slots], 1.0, 0.0), sums[:, :128],
            precision=lax.Precision.HIGHEST, preferred_element_type=jnp.float32,
        ) + jnp.dot(
            jnp.where(spot == spots[0:1, :slots] + 1, 1.0, 0.0), sums[:, 128:],
            precision=lax.Precision.HIGHEST, preferred_element_type=jnp.float32,
        )
        col_own[it] = totals.reshape(32, 8, 128)

        def scatter(d, _):
            to = lax.rem(w + d, 32)
            remote(col_own.at[it, to], col_buf.at[it, d - 1], col_send.at[it], col_recv.at[it], (to, z)).start()
            return 0

        lax.fori_loop(1, 32, scatter, 0)
        took(col_buf.at[it], col_recv.at[it])
        plane_buf[it, a] = col_own[it, w] + jnp.sum(col_buf[it], axis=0)
        for d in (1, 2, 3):
            mine = plane_buf.at[it, a]
            remote(mine, mine, plane_send.at[it], plane_recv.at[it], (w, lax.rem(z + 4 * d, 16))).start()
        took(plane_buf.at[it, pl.ds(0, 3)], plane_recv.at[it])
        column_total = (plane_buf[it, 0] + plane_buf[it, 1]) + (plane_buf[it, 2] + plane_buf[it, 3])
        scale_buf[it, w] = employer_mass[...] / column_total

        def share(d, _):
            mine = scale_buf.at[it, w]
            remote(mine, mine, scale_send.at[it], scale_recv.at[it], (lax.rem(w + d, 32), z)).start()
            return 0

        lax.fori_loop(1, 32, share, 0)
        took(scale_buf.at[it, pl.ds(0, 31)], scale_recv.at[it])

    for k in range(32):
        employer_out[2 * k : 2 * k + 2, :] = SOFTMAX_TEMP * jnp.log(scale_buf[ITERS - 1, k, pl.ds(2 * a, 2), :])
    took(out_buf.at[pl.ds(0, 3)], out_recv)
    worker_out[...] = out_buf[...].reshape(128, 128)

    took(out_buf.at[pl.ds(0, 3)], out_send)
    for it in range(ITERS):
        took(row_buf.at[it, pl.ds(0, 3)], row_send.at[it])
        took(col_buf.at[it], col_send.at[it])
        took(plane_buf.at[it, pl.ds(0, 3)], plane_send.at[it])
        took(scale_buf.at[it, pl.ds(0, 31)], scale_send.at[it])


def iterate(slots, cid, lists, rows, cols, spots, worker_mass, employer_mass):
    f32 = jnp.float32
    return pl.pallas_call(
        functools.partial(iterate_kernel, slots),
        out_shape=[jax.ShapeDtypeStruct((128, 128), f32), jax.ShapeDtypeStruct((64, 128), f32)],
        in_specs=[SMEM] + [VMEM] * 5,
        out_specs=[VMEM, VMEM],
        scratch_shapes=[
            pltpu.VMEM((slots, RW, RE), jnp.bfloat16),
            pltpu.VMEM((ITERS, 4, 4, 8, 128), f32),
            pltpu.VMEM((ITERS, 4, 8, 128), f32),
            pltpu.VMEM((slots, 1, RE), f32),
            pltpu.VMEM((ITERS, 32, 8, 128), f32),
            pltpu.VMEM((ITERS, 31, 8, 128), f32),
            pltpu.VMEM((ITERS, 4, 8, 128), f32),
            pltpu.VMEM((ITERS, 32, 8, 128), f32),
            pltpu.VMEM((4, 4, 8, 128), f32),
        ]
        + [DMA((ITERS,))] * 8
        + [DMA, DMA],
        compiler_params=pltpu.CompilerParams(
            collective_id=cid, has_side_effects=True, vmem_limit_bytes=(20 + slots // 2) << 20
        ),
        name=f"iterate_{slots}",
    )(lists, rows, cols, spots, worker_mass, employer_mass)


def shards(worker_emb, employer_emb, eligible, worker_mass, employer_mass):
    inputs = worker_emb, employer_emb, eligible, employer_mass.reshape(64, 128)
    inputs = [pltpu.with_memory_space_constraint(one, pltpu.HBM) for one in inputs]
    rows, cols, lists, spots, masses, which = gather(*inputs)
    worker_mass = worker_mass.reshape(128, 128)

    def run(slots, cid):
        return lambda: iterate(slots, cid, lists, rows, cols, spots, worker_mass, masses)

    worker_pot, employer_pot = lax.switch(which[0, 0], [run(slots, k + 1) for k, slots in enumerate(SLOTS)])
    return worker_pot.reshape(-1), employer_pot.reshape(-1)


def solution(mesh):
    return jax.shard_map(
        shards,
        mesh=mesh,
        in_specs=(P(("wrk", "emp"), None), P("wrk", "emp"), P("wrk", "emp"), P("wrk"), P("emp")),
        out_specs=(P("wrk"), P("emp")),
        check_vma=False,
    )
```

```python
import functools

import jax
import jax.numpy as jnp
from jax import lax
from jax.experimental import pallas as pl
from jax.experimental.pallas import tpu as pltpu
from jax.sharding import PartitionSpec as P

E = 256
ITERS = 3
SOFTMAX_TEMP = 0.25
EPSILON = 1e-06
RW = 1024
RE = 256
SLOTS = (13, 17, 48)
CHUNKS = 4
ORDER = (
    "Z", "o0", "o1", "f00", "f01", "f02", "f03", "f10", "f11", "f12", "f13", "s00", "s01", "R", "s10", "s11",
    "n", "o2", "o3", "t00", "t01", "t02", "t03", "t10", "t11", "t12", "t13", "f20", "f21", "f22", "f23", "f30",
    "o4", "o5", "f31", "f32", "f33", "r10", "e0", "s21", "s20", "e1", "r11", "f40", "f41", "f42", "f43", "f51",
    "s30", "s31", "f50", "f52", "f53", "r12", "t20", "t21", "t22", "t23", "s40", "s41", "r13", "m0", "t30",
    "t31", "t32", "t33", "s50", "s51", "e2", "t40", "t41", "t42", "t43", "o6", "o7", "e3", "m1", "r20", "t50",
    "t51", "t52", "t53", "r21", "e4", "f60", "f61", "f62", "f63", "f70", "f71", "f72", "f73", "r22", "m2",
    "s60", "s61", "e5", "s70", "s71", "r23", "r30", "t60", "t61", "t62", "t63", "m3", "r31", "t70", "t71",
    "t72", "t73", "e6", "r32", "e7", "r33",
)
MESH = pl.DeviceIdType.MESH
VMEM = pl.BlockSpec(memory_space=pltpu.VMEM)
SMEM = pl.BlockSpec(memory_space=pltpu.SMEM)
HBM = pl.BlockSpec(memory_space=pltpu.HBM)
DMA = pltpu.SemaphoreType.DMA


def place():
    w, z = lax.axis_index("wrk"), lax.axis_index("emp")
    return w // 8, lax.rem(w // 2, 4), lax.rem(w, 2), z // 4, lax.rem(z, 4)


def device(x, y, c, z):
    return ((lax.rem(x, 4) * 4 + lax.rem(y, 4)) * 2 + c, lax.rem(z, 16))


def remote(src, dst, send, recv, to):
    return pltpu.make_async_remote_copy(
        src_ref=src, dst_ref=dst, send_sem=send, recv_sem=recv, device_id=to, device_id_type=MESH
    )


def took(ref, sem):
    pltpu.make_async_copy(ref, ref, sem).wait()


def gather_kernel(
    wk, em_all, eligible_all, mass_all,
    rows, cols, lists, spots, masses, which,
    em, eligible, mass, shard, small_all, top, top_all,
    load_sem, keep_sem, z_send, z_recv, xy_send, xy_recv, core_send, core_recv,
    row_send, row_recv, small_send, small_recv, top_send, top_recv,
):
    x, y, c, a, b = place()
    w, z = lax.axis_index("wrk"), lax.axis_index("emp")
    left, right = device(x + 3, y, c, z), device(x + 1, y, c, z)
    down, up = device(x, y + 3, c, z), device(x, y + 1, c, z)
    back, ahead = (w, lax.rem(z + 12, 16)), (w, lax.rem(z + 4, 16))
    twin = (w + 1 - 2 * c, z)

    loads = [
        pltpu.make_async_copy(src, dst, load_sem.at[k])
        for k, (src, dst) in enumerate(((em_all, em), (eligible_all, eligible), (mass_all, mass)))
    ]
    for one in loads:
        one.start()
    barrier = pltpu.get_barrier_semaphore()
    group = [(w, 4 * a + lax.rem(b + d, 4)) for d in (1, 2, 3)]
    far = [device(x + 2, y, c, z), device(x, y + 2, c, z)]
    for to in (left, right, down, up, back, ahead, twin, *group, *far):
        pl.semaphore_signal(barrier, inc=1, device_id=to, device_id_type=MESH)

    for one in loads:
        one.wait()
    for k in range(2):
        for g in range(2):
            at = 2048 * g + 1024 * k
            for q in range(4):
                here = at + RE * q
                shard[k, g, q] = jnp.concatenate(
                    [em[:, here : here + RE], em[:, 4096 + here : 4096 + here + RE]], axis=0
                )
    small_all[a] = jnp.zeros((24, 128), jnp.float32)
    small_all[a, 0:2, :] = mass[pl.ds(2 * w, 2), :]
    small_all[a, 8:24, 0:32] = eligible[...].astype(jnp.float32)
    keep = [
        pltpu.make_async_copy(shard, cols.at[a, :, x, y, c], keep_sem.at[0]),
        pltpu.make_async_copy(wk, rows.at[b], keep_sem.at[1]),
    ]
    for one in keep:
        one.start()
    pl.semaphore_wait(barrier, 12)

    xs = [lax.rem(x + i, 4) for i in range(4)]
    ys = [lax.rem(y + i, 4) for i in range(4)]
    ps = [lax.rem(a + i, 4) for i in range(4)]
    near = (right, left, up, down)

    def part(s):
        return cols.at[ps[(0, 0, 3, 1, 3, 1, 2, 2)[s]], (0, 1, 0, 0, 1, 1, 0, 1)[s]]

    def push(src, k, kind, sem):
        remote(src, src, xy_send.at[kind, k], sem, near[k]).start()

    def lanes(ref, k):
        return ref.at[pl.ds(2 * k, 2)] if len(ref.shape) == 3 else ref.at[:, pl.ds(2 * k, 2)]

    def z_own():
        for g, to in enumerate((ahead, back)):
            remote(small_all.at[a], small_all.at[a], small_send, small_recv.at[g], to).start()
        for k in range(2):
            for g, to in enumerate((ahead, back)):
                remote(shard.at[k], cols.at[a, k, x, y, c], z_send, z_recv.at[g, k], to).start()

    def relay_small():
        few = small_all.at[ps[3]]
        took(few, small_recv.at[0])
        remote(few, few, small_send, small_recv.at[2], ahead).start()

    def own(s):
        got = part(s).at[x, y, c]
        if 2 <= s < 6:
            g, k = s % 2, s // 4
            took(got, z_recv.at[g, k])
            if g == k:
                remote(got, got, z_send, z_recv.at[2, k], (ahead, back)[g]).start()
        if s >= 6:
            took(got, z_recv.at[2, s - 6])
        for k in range(4):
            src = shard.at[s, k // 2] if s < 2 else got.at[k // 2]
            remote(src, got.at[k // 2], xy_send.at[0, k], xy_recv.at[s, k], near[k]).start()
        if s == 1:
            keep[0].wait()

    def first(s, k):
        i, j = ((3, 0), (1, 0), (0, 3), (0, 1))[k]
        got = part(s).at[xs[i], ys[j], c, k // 2]
        took(got, xy_recv.at[s, k])
        push(lanes(got, k % 2), k, 1, xy_recv.at[s, 4 + k // 2])

    def to_twin(line):
        remote(line, line, core_send, core_recv, twin).start()

    def second(s, axis):
        took(part(s).at[x, y, c, axis], xy_recv.at[s, 4 + axis])
        line = part(s).at[:, y, c, 0] if axis == 0 else part(s).at[x, :, c, 1]
        for k in range(2):
            push(line, 2 - 2 * axis + k, 2, xy_recv.at[s, 6 + 2 * axis + k])
        to_twin(line)

    def third(s, k):
        line = part(s).at[:, ys[3 - 2 * k], c, 0] if k < 2 else part(s).at[xs[7 - 2 * k], :, c, 1]
        took(line, xy_recv.at[s, 6 + k])
        push(lanes(line, k % 2), (2, 3, 0, 1)[k], 3, xy_recv.at[s, 10 + k // 2])
        to_twin(line)

    def finish(s):
        for k, line in enumerate((part(s).at[:, ys[2], c, 0], part(s).at[xs[2], :, c, 1])):
            took(line, xy_recv.at[s, 10 + k])
            to_twin(line)

    def row_chunk(block, j):
        return block.at[pl.ds(j * (RW // CHUNKS), RW // CHUNKS)]

    def send_rows():
        for j in range(CHUNKS):
            src = row_chunk(wk, j)

            @pl.when(b < 3)
            def _():
                remote(src, row_chunk(rows.at[b], j), row_send.at[0, 0], row_recv.at[0, 0, j], (w, z + 1)).start()

            @pl.when(b > 0)
            def _():
                remote(src, row_chunk(rows.at[b], j), row_send.at[1, 0], row_recv.at[1, 0, j], (w, z - 1)).start()

    def relay(d, j):
        @pl.when(b >= d)
        def _():
            took(row_chunk(rows.at[b - d], j), row_recv.at[0, d - 1, j])

        if d < 3:

            @pl.when((b >= d) & (b < 3))
            def _():
                got = row_chunk(rows.at[b - d], j)
                remote(got, got, row_send.at[0, d], row_recv.at[0, d, j], (w, z + 1)).start()

        @pl.when(b + d <= 3)
        def _():
            took(row_chunk(rows.at[b + d], j), row_recv.at[1, d - 1, j])

        if d < 3:

            @pl.when((b + d <= 3) & (b > 0))
            def _():
                got = row_chunk(rows.at[b + d], j)
                remote(got, got, row_send.at[1, d], row_recv.at[1, d, j], (w, z - 1)).start()

    def list_tiles():
        took(small_all.at[0], small_recv.at[1])
        took(small_all.at[0], small_recv.at[2])
        masses[...] = small_all[:, 0:2, :].reshape(8, 128)
        flags = small_all[:, 8:24, :].reshape(64, 128)
        line = lax.broadcasted_iota(jnp.int32, (64, 128), 0)
        lane = lax.broadcasted_iota(jnp.int32, (64, 128), 1)
        group = lax.rem(line, 16) // 4
        most = jnp.zeros((1, 1), jnp.float32)
        for g in range(4):
            most = jnp.maximum(most, jnp.sum(jnp.where(group == g, flags, 0.0), keepdims=True))
        top[0] = jnp.broadcast_to(most, (8, 128))
        mine = jnp.where(group == a, flags, 0.0)
        upto = (
            lax.broadcasted_iota(jnp.int32, (128, 128), 0) <= lax.broadcasted_iota(jnp.int32, (128, 128), 1)
        ).astype(jnp.float32)
        above = (
            lax.broadcasted_iota(jnp.int32, (64, 64), 1) < lax.broadcasted_iota(jnp.int32, (64, 64), 0)
        ).astype(jnp.float32)
        before = jnp.sum(jnp.dot(above, mine, preferred_element_type=jnp.float32), axis=1, keepdims=True)
        order = jnp.dot(mine, upto, preferred_element_type=jnp.float32) + before
        slot = lane.astype(jnp.float32)
        ends = before + jnp.sum(mine, axis=1, keepdims=True)
        slot_line = jnp.sum(jnp.where(ends <= slot, 1.0, 0.0), axis=0, keepdims=True)
        hit = jnp.where(line.astype(jnp.float32) == slot_line, 1.0, 0.0)
        there = lax.dot_general(order, hit, (((0,), (0,)), ((), ())), preferred_element_type=jnp.float32)
        slot_lane = jnp.sum(jnp.where(there <= slot[0:1], 1.0, 0.0), axis=0, keepdims=True)
        count = jnp.sum(mine, keepdims=True)
        codes = jnp.where(slot[0:1] < count, slot_line * 32.0 + slot_lane, 0.0).astype(jnp.int32)
        count = jnp.broadcast_to(count, (1, 128)).astype(jnp.int32)
        plane, row, col = codes // 512, lax.rem(codes // 32, 4), lax.rem(codes, 32)
        at = lax.broadcasted_iota(jnp.int32, (8, 128), 0)
        fields = (
            row, plane, col, count, lax.rem(col // 4, 2), lax.rem(col // 8, 2), lax.rem(col, 4), col // 16,
        )
        table = jnp.zeros((8, 128), jnp.int32)
        for k, field in enumerate(fields):
            table = jnp.where(at == k, field, table)
        lists[...] = table
        spots[...] = jnp.broadcast_to(col * 8 + plane * 2, (8, 128))

    circles = (
        [device(x + d, y, c, z) for d in (1, 2, 3)],
        [device(x, y + d, c, z) for d in (1, 2, 3)],
        group,
        [twin],
    )

    def maximum(k):
        if k == 0:
            list_tiles()
        else:
            for d in range(3):
                took(top_all.at[k - 1, d], top_recv.at[k - 1, d])
            top[k] = jnp.maximum(top[k - 1], jnp.max(top_all[k - 1], axis=0))
        for d, to in enumerate(circles[k]):
            remote(top.at[k], top_all.at[k, d], top_send.at[k, d], top_recv.at[k, d], to).start()

    steps = dict(
        m=maximum, n=relay_small,
        Z=z_own, o=own, f=first, s=second, t=third, e=finish, R=send_rows, r=relay,
    )
    for step in ORDER:
        steps[step[0]](*map(int, step[1:]))

    took(top_all.at[3, 0], top_recv.at[3, 0])
    most = jnp.max(jnp.maximum(top[3], top_all[3, 0]))
    which[0, 0] = sum(jnp.where(most > slots, 1, 0) for slots in SLOTS[:-1]).astype(jnp.int32)

    keep[1].wait()
    took(cols.at[pl.ds(0, 2)], core_recv)
    took(cols.at[pl.ds(0, 2)], core_send)
    for k in range(4):
        took(cols.at[0, 0, 0, pl.ds(0, 2)], xy_send.at[0, k])
        took(cols.at[0, 0, 0, 0], xy_send.at[1, k])
        took(cols.at[0, 0, pl.ds(0, 2)], xy_send.at[2, k])
        took(cols.at[0, 0, 0], xy_send.at[3, k])
    took(cols.at[0, 0, 0, pl.ds(0, 3)], z_send)
    took(small_all.at[pl.ds(0, 3)], small_send)
    for k in range(4):
        for d in range(len(circles[k])):
            took(top.at[k], top_send.at[k, d])

    for d in range(3):

        @pl.when((b >= d) & (b < 3))
        def _():
            took(rows.at[0], row_send.at[0, d])

        @pl.when((b + d <= 3) & (b > 0))
        def _():
            took(rows.at[0], row_send.at[1, d])


def gather(wk, em, eligible, mass):
    f32 = jnp.float32
    return pl.pallas_call(
        gather_kernel,
        out_shape=[
            jax.ShapeDtypeStruct((4, RW, E), jnp.bfloat16),
            jax.ShapeDtypeStruct((4, 2, 4, 4, 2, 2, 4, 16, RE), jnp.bfloat16),
            jax.ShapeDtypeStruct((8, 128), jnp.int32),
            jax.ShapeDtypeStruct((8, 128), jnp.int32),
            jax.ShapeDtypeStruct((8, 128), f32),
            jax.ShapeDtypeStruct((1, 1), jnp.int32),
        ],
        in_specs=[HBM] * 4,
        out_specs=[VMEM] * 5 + [SMEM],
        scratch_shapes=[
            pltpu.VMEM((8, 8192), jnp.bfloat16),
            pltpu.VMEM((16, 32), jnp.int32),
            pltpu.VMEM((64, 128), f32),
            pltpu.VMEM((2, 2, 4, 16, RE), jnp.bfloat16),
            pltpu.VMEM((4, 24, 128), f32),
            pltpu.VMEM((4, 8, 128), f32),
            pltpu.VMEM((4, 3, 8, 128), f32),
            DMA((3,)), DMA((2,)), DMA, DMA((3, 2)), DMA((4, 4)), DMA((8, 12)), DMA, DMA,
            DMA((2, 3)), DMA((2, 3, CHUNKS)), DMA, DMA((3,)), DMA((4, 3)), DMA((4, 3)),
        ],
        compiler_params=pltpu.CompilerParams(collective_id=0, has_side_effects=True, vmem_limit_bytes=24 << 20),
        name="gather",
    )(wk, em, eligible, mass)


def build_tile(t, lists, rows, cols, tiles):
    row = lists[0, t]
    keep = jnp.where(jnp.full((1, RE), lists[3, t], jnp.int32) > t, 1.0, 0.0)
    both = cols[lists[1, t], lists[4, t], :, :, :, lists[5, t], lists[6, t], :, :]
    both = both.reshape(32, 16, RE).astype(jnp.float32)
    upper = jnp.full((32, 8, RE), lists[7, t], jnp.int32) == 1
    side = jnp.where(upper, both[:, 8:, :], both[:, :8, :]).reshape(E, RE)
    inv_cols = lax.rsqrt(jnp.sum(side * side, axis=0, keepdims=True) * (1.0 / E) + EPSILON)
    inv_cols = inv_cols * (1.0 / E)
    side = side.astype(jnp.bfloat16)
    for j in range(RW // 256):
        part = rows[row, pl.ds(j * 256, 256), :]
        wide = part.astype(jnp.float32)
        inv_rows = lax.rsqrt(jnp.sum(wide * wide, axis=1, keepdims=True) * (1.0 / E) + EPSILON)
        cosine = jnp.dot(part, side, preferred_element_type=jnp.float32) * inv_rows * inv_cols
        value = jnp.exp((cosine - 1.0) * (1.0 / SOFTMAX_TEMP)) * keep
        tiles[t, pl.ds(j * 256, 256), :] = value.astype(jnp.bfloat16)


def in_line(block, lines):
    return jnp.concatenate([jnp.broadcast_to(block[k : k + 1], (16, 128)) for k in lines], axis=1)


def stacked(vector):
    at = lax.broadcasted_iota(jnp.int32, (8, 128), 0)
    out = jnp.zeros((8, 128), jnp.float32)
    for k in range(8):
        out = jnp.where(at == k, vector[:, 128 * k : 128 * k + 128], out)
    return out


def in_two(wide):
    high = wide.astype(jnp.bfloat16).astype(jnp.float32)
    at = lax.broadcasted_iota(jnp.int32, wide.shape, 0)
    return jnp.where(at == 0, high, jnp.where(at == 1, wide - high, 0.0)).astype(jnp.bfloat16)


def placed(matrix, values):
    high = values.astype(jnp.bfloat16)
    rest = values - high.astype(jnp.float32)
    middle = rest.astype(jnp.bfloat16)
    low = (rest - middle.astype(jnp.float32)).astype(jnp.bfloat16)
    parts = jnp.concatenate([high, middle, low], axis=1)
    out = jnp.dot(matrix, parts, preferred_element_type=jnp.float32)
    return (out[:, :128] + out[:, 128:256]) + out[:, 256:]


def iterate_kernel(
    slots,
    lists, rows, cols, spots, worker_mass, employer_mass,
    worker_out, employer_out,
    tiles, row_buf, worker_scale, part, col_own, col_buf, plane_buf, scale_buf, out_buf,
    row_send, row_recv, col_send, col_recv, plane_send, plane_recv,
    scale_send, scale_recv, out_send, out_recv,
):
    x, y, c, a, b = place()
    w, z = lax.axis_index("wrk"), lax.axis_index("emp")
    barrier = pltpu.get_barrier_semaphore()

    def greet_w(d, _):
        pl.semaphore_signal(barrier, inc=1, device_id=(lax.rem(w + d, 32), z), device_id_type=MESH)
        return 0

    lax.fori_loop(1, 32, greet_w, 0)
    for d in (1, 2, 3):
        pl.semaphore_signal(barrier, inc=1, device_id=(w, lax.rem(z + 4 * d, 16)), device_id_type=MESH)
        pl.semaphore_signal(barrier, inc=1, device_id=(w, 4 * a + lax.rem(b + d, 4)), device_id_type=MESH)

    def build_step(t, _):
        build_tile(t, lists, rows, cols, tiles)
        return 0

    lax.fori_loop(0, slots, build_step, 0)
    unroll = slots if slots <= 20 else 4
    spot = lax.broadcasted_iota(jnp.int32, (256, slots), 0)
    to_first = jnp.where(spot == spots[0:1, :slots], 1.0, 0.0).astype(jnp.bfloat16)
    to_second = jnp.where(spot == spots[0:1, :slots] + 1, 1.0, 0.0).astype(jnp.bfloat16)
    block_line = lax.broadcasted_iota(jnp.int32, (8, 128), 0)

    for it in range(ITERS):

        def row_step(t, totals):
            if it == 0:
                scale = jnp.ones((16, RE), jnp.float32)
            else:
                block = scale_buf[it - 1, lists[2, t]]
                line = 2 * lists[1, t]
                first = jnp.sum(jnp.where(block_line == line, block, 0.0), axis=0, keepdims=True)
                second = jnp.sum(jnp.where(block_line == line + 1, block, 0.0), axis=0, keepdims=True)
                scale = jnp.broadcast_to(jnp.concatenate([first, second], axis=1), (16, RE))
            sums = lax.dot_general(
                in_two(scale), tiles[t], (((1,), (1,)), ((), ())), preferred_element_type=jnp.float32
            )
            sums = stacked(sums[0:1] + sums[1:2])
            row = jnp.full((8, 128), lists[0, t], jnp.int32)
            return tuple(total + jnp.where(row == r, sums, 0.0) for r, total in enumerate(totals))

        totals = lax.fori_loop(0, slots, row_step, (jnp.zeros((8, 128), jnp.float32),) * 4, unroll=unroll)
        for r in range(4):
            row_buf[it, b, r] = totals[r]
        if it == 0:
            pl.semaphore_wait(barrier, 37)
        for d in (1, 2, 3):
            mine = row_buf.at[it, b]
            remote(mine, mine, row_send.at[it], row_recv.at[it], (w, 4 * a + lax.rem(b + d, 4))).start()
        took(row_buf.at[it, pl.ds(0, 3)], row_recv.at[it])
        row_total = (row_buf[it, 0] + row_buf[it, 1]) + (row_buf[it, 2] + row_buf[it, 3])
        mass = worker_mass[pl.ds(pl.multiple_of(32 * a, 32), 32), :].reshape(4, 8, 128)
        worker_scale[it] = mass / row_total
        if it == ITERS - 1:
            out_buf[a] = SOFTMAX_TEMP * jnp.log(worker_scale[it])
            for d in (1, 2, 3):
                remote(out_buf.at[a], out_buf.at[a], out_send, out_recv, (w, lax.rem(z + 4 * d, 16))).start()

        def col_step(t, _):
            scale = in_line(worker_scale[it, lists[0, t]], range(8))
            sums = jnp.dot(in_two(scale), tiles[t], preferred_element_type=jnp.float32)
            part[t] = sums[0:1] + sums[1:2]
            return 0

        lax.fori_loop(0, slots, col_step, 0, unroll=unroll)
        sums = part[...].reshape(slots, RE)
        totals = placed(to_first, sums[:, :128]) + placed(to_second, sums[:, 128:])
        col_own[it] = totals.reshape(32, 8, 128)

        def scatter(d, _):
            to = lax.rem(w + d, 32)
            remote(col_own.at[it, to], col_buf.at[it, d - 1], col_send.at[it], col_recv.at[it], (to, z)).start()
            return 0

        lax.fori_loop(1, 32, scatter, 0)
        took(col_buf.at[it], col_recv.at[it])
        plane_buf[it, a] = col_own[it, w] + jnp.sum(col_buf[it], axis=0)
        for d in (1, 2, 3):
            mine = plane_buf.at[it, a]
            remote(mine, mine, plane_send.at[it], plane_recv.at[it], (w, lax.rem(z + 4 * d, 16))).start()
        took(plane_buf.at[it, pl.ds(0, 3)], plane_recv.at[it])
        column_total = (plane_buf[it, 0] + plane_buf[it, 1]) + (plane_buf[it, 2] + plane_buf[it, 3])
        scale_buf[it, w] = employer_mass[...] / column_total

        def share(d, _):
            mine = scale_buf.at[it, w]
            remote(mine, mine, scale_send.at[it], scale_recv.at[it], (lax.rem(w + d, 32), z)).start()
            return 0

        lax.fori_loop(1, 32, share, 0)
        took(scale_buf.at[it, pl.ds(0, 31)], scale_recv.at[it])

    for k in range(32):
        employer_out[2 * k : 2 * k + 2, :] = SOFTMAX_TEMP * jnp.log(scale_buf[ITERS - 1, k, pl.ds(2 * a, 2), :])
    took(out_buf.at[pl.ds(0, 3)], out_recv)
    worker_out[...] = out_buf[...].reshape(128, 128)

    took(out_buf.at[pl.ds(0, 3)], out_send)
    for it in range(ITERS):
        took(row_buf.at[it, pl.ds(0, 3)], row_send.at[it])
        took(col_buf.at[it], col_send.at[it])
        took(plane_buf.at[it, pl.ds(0, 3)], plane_send.at[it])
        took(scale_buf.at[it, pl.ds(0, 31)], scale_send.at[it])


def iterate(slots, cid, lists, rows, cols, spots, worker_mass, employer_mass):
    f32 = jnp.float32
    return pl.pallas_call(
        functools.partial(iterate_kernel, slots),
        out_shape=[jax.ShapeDtypeStruct((128, 128), f32), jax.ShapeDtypeStruct((64, 128), f32)],
        in_specs=[SMEM] + [VMEM] * 5,
        out_specs=[VMEM, VMEM],
        scratch_shapes=[
            pltpu.VMEM((slots, RW, RE), jnp.bfloat16),
            pltpu.VMEM((ITERS, 4, 4, 8, 128), f32),
            pltpu.VMEM((ITERS, 4, 8, 128), f32),
            pltpu.VMEM((slots, 1, RE), f32),
            pltpu.VMEM((ITERS, 32, 8, 128), f32),
            pltpu.VMEM((ITERS, 31, 8, 128), f32),
            pltpu.VMEM((ITERS, 4, 8, 128), f32),
            pltpu.VMEM((ITERS, 32, 8, 128), f32),
            pltpu.VMEM((4, 4, 8, 128), f32),
        ]
        + [DMA((ITERS,))] * 8
        + [DMA, DMA],
        compiler_params=pltpu.CompilerParams(
            collective_id=cid, has_side_effects=True, vmem_limit_bytes=(20 + slots // 2) << 20
        ),
        name=f"iterate_{slots}",
    )(lists, rows, cols, spots, worker_mass, employer_mass)


def shards(worker_emb, employer_emb, eligible, worker_mass, employer_mass):
    inputs = worker_emb, employer_emb, eligible, employer_mass.reshape(64, 128)
    inputs = [pltpu.with_memory_space_constraint(one, pltpu.HBM) for one in inputs]
    rows, cols, lists, spots, masses, which = gather(*inputs)
    worker_mass = worker_mass.reshape(128, 128)

    def run(slots, cid):
        return lambda: iterate(slots, cid, lists, rows, cols, spots, worker_mass, masses)

    worker_pot, employer_pot = lax.switch(which[0, 0], [run(slots, k + 1) for k, slots in enumerate(SLOTS)])
    return worker_pot.reshape(-1), employer_pot.reshape(-1)


def solution(mesh):
    return jax.shard_map(
        shards,
        mesh=mesh,
        in_specs=(P(("wrk", "emp"), None), P("wrk", "emp"), P("wrk", "emp"), P("wrk"), P("emp")),
        out_specs=(P("wrk"), P("emp")),
        check_vma=False,
    )
```
